256 devices in a mesh: tok: 4 (over z_lo, core), voc: 64 (over z_hi, y, x).
Axes of the slice: x: 4, y: 4, z: 8 (z_hi: 4, z_lo: 2; z = z_hi * 2 + z_lo), core: 2. Of those that a mesh axis runs over, the one named last changes fastest.
Arguments:
- hidden_states: bfloat16 [1024, 3584], P('tok'), may hold values from -12 to 12
- student_head: bfloat16 [3584, 131072], P('tok', 'voc'), may hold values from -0.5 to 0.5
- teacher_logits: bfloat16 [1024, 131072], P(('tok', 'voc')), may hold values from -16 to 320
- quality: float32 [1024], P('tok'), may hold values from 0.25 to 4
Outputs:
- hidden_grad: bfloat16 [1024, 3584], P('tok', 'voc')
- head_grad: bfloat16 [3584, 131072], P('tok', 'voc')
The draws below stay inside these ranges and needn't reach their ends.
All inputs are finite; a program needn't handle non-finite values.
Results may differ from the reference program's by a relative error of at most 0.0121.
Values may be sent and summed in bfloat16 or wider, within the bound.
A program may use at most 128 MiB of HBM per device.

```python
import math
import jax
import jax.numpy as jnp
from jax import lax

D = 3584
TOK_DEV = 256
VOCAB = 131072
TOKENS = 1024
N_TOK = 4


def head_matrix(key, ramp):
    base = jax.random.normal(jax.random.fold_in(key, 101), (D, VOCAB), jnp.float32)
    spread = jnp.exp(jax.random.uniform(jax.random.fold_in(key, 102), (1, VOCAB), jnp.float32, math.log(0.7), math.log(1.4)))
    column = jnp.arange(VOCAB, dtype=jnp.float32)[None, :] / VOCAB
    return jnp.clip(base * 0.05 * spread * (1.0 + ramp * column), -0.5, 0.5)


def draw_student_head(key, part):
    ramp = 0.12
    return head_matrix(key, ramp).astype(jnp.bfloat16)


def draw_hidden_states(key, part):
    key = jax.random.fold_in(key, 7)
    keys = jax.random.split(key, 2)
    drawn = jax.random.normal(keys[0], (TOKENS, D), jnp.float32)
    scales = jnp.exp(jax.random.uniform(keys[1], (TOKENS, 1), jnp.float32, math.log(0.4), math.log(2.5)))
    values = drawn * scales
    return jnp.clip(values, -12.0, 12.0).astype(jnp.bfloat16)


def draw_teacher_logits(key, part):
    key = jax.random.fold_in(key, 9)
    keys = jax.random.split(key, 1)
    column = jnp.arange(VOCAB, dtype=jnp.float32)[None, :] / VOCAB
    values = jnp.clip(jax.random.normal(keys[0], (TOKENS, VOCAB), jnp.float32) * 3.0 * (1.0 + 0.12 * column), -16.0, 16.0)
    return values.astype(jnp.bfloat16)


def shard_levels(stream_key, dims, shards, least, largest):
    loudness = 1.0
    for position, shards_of in shards:
        heights = jax.random.uniform(jax.random.fold_in(jax.random.fold_in(stream_key, 6), position), (shards_of,), jnp.float32, least / len(shards), largest / len(shards))
        loudness = loudness * jnp.repeat(jnp.exp(heights), dims[position] // shards_of).reshape((-1,) + (1,) * (len(dims) - 1 - position))
    return loudness


def setup_inputs(seed: int = 0) -> dict:
    key_list = jax.random.split(jax.random.key(seed), 5)
    hidden_states = draw_hidden_states(jax.random.fold_in(key_list[4], 71), 0)
    student_head = draw_student_head(jax.random.fold_in(key_list[4], 71), 0)
    teacher_logits = draw_teacher_logits(jax.random.fold_in(key_list[4], 71), 0)
    quality = jnp.clip(jnp.exp(math.log(4.0) - 2.7725887 * jax.random.uniform(key_list[3], (TOKENS,), jnp.float32) ** shard_levels(key_list[3], (TOKENS,), ((0, 4),), -0.2, 0.2)), 0.25, 4.0)
    return dict(hidden_states=hidden_states, student_head=student_head, teacher_logits=teacher_logits, quality=quality)


loss_scale = 64.0


def row_lse(logits):
    top = jnp.max(logits, axis=1, keepdims=True)
    return top + jnp.log(jnp.sum(jnp.exp(logits - top), axis=1, keepdims=True))


def reference(hidden_states, student_head, teacher_logits, quality):
    student = jnp.dot(hidden_states, student_head, preferred_element_type=jnp.float32)
    student_lse = row_lse(student)
    teacher = teacher_logits.astype(jnp.float32)
    teacher_lse = row_lse(teacher)
    diff = jnp.exp(student - student_lse) - jnp.exp(teacher - teacher_lse)
    grads = (loss_scale * quality[:, None] * diff).astype(jnp.bfloat16)
    hidden_grad = lax.dot_general(grads, student_head, (((1,), (1,)), ((), ())), preferred_element_type=jnp.float32).astype(jnp.bfloat16)
    hidden_groups = hidden_states.reshape(N_TOK, TOK_DEV, D)
    grad_groups = grads.reshape(N_TOK, TOK_DEV, VOCAB)

    def add_group(carry, pair):
        group_hidden, group_grads = pair
        term = lax.dot_general(group_hidden, group_grads, (((0,), (0,)), ((), ())), preferred_element_type=jnp.float32)
        rounded = lax.optimization_barrier(term.astype(jnp.bfloat16))
        return carry + rounded.astype(jnp.float32), None

    total, unused = lax.scan(add_group, jnp.zeros((D, VOCAB), jnp.float32), (hidden_groups, grad_groups))
    return hidden_grad, total.astype(jnp.bfloat16)
```

```python
import functools

import jax
import jax.numpy as jnp
from jax import lax
from jax.experimental import pallas as pl
from jax.experimental.pallas import tpu as pltpu
from jax.sharding import PartitionSpec as P

MESH = pl.DeviceIdType.MESH
LOSS_SCALE = 64.0
D = 3584
DS = 896
TOK = 1024
TG = 256
COLS = 512
BLK = 128
NB = 8
ROWS = 56
CHUNKS = ((0, 256), (256, 256), (512, 256), (768, 128))
F32 = jnp.float32
BF16 = jnp.bfloat16


def mult(x, m):
    return pl.multiple_of(x, m)


def kernel(
    hid, head, teach, qual, hg, gh,
    hid_all, headv, hcols, tloc, ta, tb, stu, gs, hid_t, acc, stage,
    pb, r1, s1, r2, s2, fin, msg_a, got_a, msg_b, got_b, planes,
    loc, head_s, head_r, hid_s, hid_r, bc_s, bc_r, ta_s, ta_r, tb_s, tb_r,
    la_s, la_r, lb_s, lb_r, g_s, g_r, r1_s, r1_r, r2_s, r2_r, f_s, f_r, out_s,
):
    t = lax.axis_index("tok")
    v = lax.axis_index("voc")
    z = v // 16
    p = v % 16
    y = p // 4
    x = p % 4
    c = t // 2
    h = t % 2
    sib = c * 2 + (1 - h)
    cross = (1 - c) * 2 + h
    diag = (1 - c) * 2 + (1 - h)
    tz = t * 4 + z

    def plane_peer(k):
        return (t, z * 16 + lax.rem(p + k, 16))

    def tz_peer(k):
        q = lax.rem(tz + k, 16)
        return (q // 4, (q % 4) * 16 + p)

    def remote(src, dst, ss, rs, dev):
        return pltpu.make_async_remote_copy(
            src_ref=src, dst_ref=dst, send_sem=ss, recv_sem=rs, device_id=dev, device_id_type=MESH
        )

    def arrived(ref, sem):
        pltpu.make_async_copy(ref, ref, sem).wait()

    bar = pltpu.get_barrier_semaphore()

    def greet(k, _):
        pl.semaphore_signal(bar, inc=1, device_id=plane_peer(k), device_id_type=MESH)
        pl.semaphore_signal(bar, inc=1, device_id=tz_peer(k), device_id_type=MESH)
        return 0

    lax.fori_loop(1, 16, greet, 0)

    c_own = pltpu.make_async_copy(head.at[:, pl.ds(mult(COLS * t, COLS), COLS)], hcols.at[t], loc.at[0])
    c_hid = pltpu.make_async_copy(hid, hid_all.at[pl.ds(mult(TG * t, TG), TG)], loc.at[1])
    c_head = pltpu.make_async_copy(head, headv, loc.at[2])
    c_tl = pltpu.make_async_copy(teach, tloc, loc.at[3])
    c_ta = pltpu.make_async_copy(teach.at[:, p], ta.at[p // 2, p % 2], loc.at[4])
    for cp in (c_hid, c_own, c_tl, c_ta, c_head):
        cp.start()

    pl.semaphore_wait(bar, 30)

    def piece(group, q):
        return (
            pl.ds(mult(TG * group + 16 * (q // 2), 16), 16),
            pl.ds(mult(1792 * (q % 2), 128), 1792),
        )

    pr, pc = piece(0, p)
    mr, mc = piece(t, p)
    h_cross = remote(hid.at[pr, pc], hid_all.at[mr, mc], hid_s.at[0], hid_r.at[0], (cross, v))
    h_cross.start()
    znb = lax.rem(z + 2 * c + 3, 4)
    h_pair = remote(
        hid.at[pl.ds(128, 128)], hid_all.at[pl.ds(mult(TG * t + 128, 128), 128)],
        hid_s.at[1], hid_r.at[1], (cross, znb * 16 + p),
    )
    h_sib = remote(
        hid, hid_all.at[pl.ds(mult(TG * t, TG), TG)], hid_s.at[2], hid_r.at[2], (sib, v)
    )
    heads = []
    for i, (r0, rn) in enumerate(CHUNKS):
        for j, dev in enumerate((cross, diag, sib)):
            heads.append(
                remote(
                    head.at[pl.ds(r0, rn), pl.ds(mult(COLS * dev, COLS), COLS)],
                    hcols.at[t, pl.ds(r0, rn)],
                    head_s.at[i, j], head_r.at[t, i], (dev, v),
                )
            )
    for cp in heads[:3]:
        cp.start()
    h_pair.start()
    h_sib.start()
    for cp in heads[3:]:
        cp.start()

    xr, xc = piece(cross, p)
    arrived(hid_all.at[xr, xc], hid_r.at[0])

    def spread_copy(k):
        return remote(
            hid_all.at[xr, xc], hid_all.at[xr, xc], bc_s.at[k - 1], bc_r.at[k - 1], plane_peer(k)
        )

    def ta_copy(k):
        q = lax.rem(p + k, 16)
        return remote(
            teach.at[:, q], ta.at[p // 2, p % 2], ta_s.at[k - 1], ta_r.at[k - 1], plane_peer(k)
        )

    def start_spread(k, _):
        spread_copy(k).start()
        return 0

    def start_ta(k, _):
        ta_copy(k).start()
        return 0

    lax.fori_loop(1, 16, start_spread, 0)
    lax.fori_loop(1, 16, start_ta, 0)

    c_tl.wait()

    def tl_tile(i):
        return tloc[i // 4, pl.ds(mult((i % 4) * 4, 4), 4)].astype(F32)

    def top_step(i, m):
        return jnp.maximum(m, jnp.max(tl_tile(i), axis=(0, 1)))

    top16 = lax.fori_loop(0, 16, top_step, jnp.full((16, 128), -jnp.inf, F32))
    top16 = jnp.max(top16, axis=1, keepdims=True)
    top4 = jnp.maximum(jnp.maximum(top16[0:4], top16[4:8]), jnp.maximum(top16[8:12], top16[12:16]))
    top16 = jnp.concatenate([top4] * 4, axis=0)
    top_full = jnp.broadcast_to(top16, (16, 128))

    def sum_step(i, s):
        return s + jnp.sum(jnp.exp(tl_tile(i) - top_full), axis=(0, 1))

    sum16 = lax.fori_loop(0, 16, sum_step, jnp.zeros((16, 128), F32))
    sum16 = jnp.sum(sum16, axis=1, keepdims=True)
    sum4 = sum16[0:4] + sum16[4:8] + sum16[8:12] + sum16[12:16]
    lse4 = top4 + jnp.log(sum4)
    row = lax.broadcasted_iota(jnp.int32, (8, 128), 0)
    lane = lax.broadcasted_iota(jnp.int32, (8, 128), 1)
    tplane = jnp.zeros((8, 128), F32)
    for r in range(4):
        here = (row == 2 * t + v // 32) & (lane == 4 * lax.rem(v, 32) + r)
        tplane = jnp.where(here, jnp.broadcast_to(lse4[r : r + 1], (8, 128)), tplane)
    msg_a[2] = tplane

    gx = mult(TG * cross, TG)

    def wait_spread(k, _):
        ar, ac = piece(cross, lax.rem(p + 16 - k, 16))
        arrived(hid_all.at[ar, ac], bc_r.at[k - 1])
        return 0

    lax.fori_loop(1, 16, wait_spread, 0)
    fwd1 = remote(
        hid_all.at[pl.ds(gx, 128)], hid_all.at[pl.ds(gx, 128)], hid_s.at[3], hid_r.at[3], (sib, v)
    )
    fwd1.start()
    gx2 = mult(TG * cross + 128, 128)
    arrived(hid_all.at[pl.ds(gx2, 128)], hid_r.at[1])
    fwd2 = remote(
        hid_all.at[pl.ds(gx2, 128)], hid_all.at[pl.ds(gx2, 128)], hid_s.at[4], hid_r.at[4], (sib, v)
    )
    fwd2.start()
    c_hid.wait()
    arrived(hid_all.at[pl.ds(mult(TG * sib, TG), TG)], hid_r.at[2])
    arrived(hid_all.at[pl.ds(mult(TG * diag, 128), 128)], hid_r.at[3])
    arrived(hid_all.at[pl.ds(mult(TG * diag + 128, 128), 128)], hid_r.at[4])

    def multiply(slot, r0, rn, first):
        base = mult(DS * slot + r0, 128)

        def step(m, _):
            rows = pl.ds(mult(m * 256, 256), 256)
            term = jnp.dot(
                hid_all[rows, pl.ds(base, rn)], hcols[slot, pl.ds(r0, rn), :],
                preferred_element_type=F32,
            )
            if first:
                stu[rows, :] = term
            else:
                stu[rows, :] += term
            return 0

        lax.fori_loop(0, 4, step, 0)

    def wait_head(slot, i):
        r0, rn = CHUNKS[i]
        arrived(hcols.at[slot, pl.ds(r0, rn)], head_r.at[slot, i])

    c_own.wait()
    multiply(t, 0, DS, True)
    for i in range(4):
        wait_head(sib, i)
    multiply(sib, 0, DS, False)

    def turn(i, _):
        rows = pl.ds(mult(i * 128, 128), 128)
        for j in range(7):
            block = hid_all[rows, pl.ds(mult(DS * t + 128 * j, 128), 128)]
            hid_t[128 * j : 128 * (j + 1), rows] = block.astype(F32).T.astype(BF16)
        return 0

    lax.fori_loop(0, 8, turn, 0)

    for i in range(3):
        r0, rn = CHUNKS[i]
        wait_head(cross, i)
        multiply(cross, r0, rn, False)
        wait_head(diag, i)
        multiply(diag, r0, rn, False)

    c_ta.wait()

    def wait_ta(k, _):
        q = lax.rem(p + 16 - k, 16)
        arrived(ta.at[q // 2, q % 2], ta_r.at[k - 1])
        return 0

    lax.fori_loop(1, 16, wait_ta, 0)
    wait_head(cross, 3)
    wait_head(diag, 3)
    for cp in heads:
        cp.wait_send()

    def tb_copy(k):
        q = lax.rem(tz + k, 16)
        return remote(
            ta.at[:, :, q % 4, q // 4], tb.at[tz], tb_s.at[k], tb_r.at[tz], tz_peer(k)
        )

    def start_tb(k, _):
        tb_copy(k).start()
        return 0

    lax.fori_loop(1, 16, start_tb, 0)
    c_tb = pltpu.make_async_copy(ta.at[:, :, z, t], tb.at[tz], tb_r.at[tz])
    c_tb.start()

    r0, rn = CHUNKS[3]
    multiply(cross, r0, rn, False)
    multiply(diag, r0, rn, False)

    def stats(b, _):
        rows = pl.ds(mult(b * BLK, BLK), BLK)
        val = stu[rows, :]
        top = jnp.max(val, axis=1, keepdims=True)
        e = jnp.exp(val - top)
        stu[rows, :] = e
        tot = jnp.sum(e, axis=1, keepdims=True)
        msg_a[0, pl.ds(b, 1), :] = jnp.broadcast_to(top, (BLK, BLK)).T[0:1, :]
        msg_a[1, pl.ds(b, 1), :] = jnp.broadcast_to(tot, (BLK, BLK)).T[0:1, :]
        return 0

    lax.fori_loop(0, NB, stats, 0)

    def la_copy(k):
        return remote(msg_a, got_a.at[k - 1], la_s.at[k - 1], la_r.at[k - 1], plane_peer(k))

    def lb_copy(k):
        return remote(msg_b, got_b.at[k - 1], lb_s.at[k - 1], lb_r.at[k - 1], tz_peer(k))

    def start_la(k, _):
        la_copy(k).start()
        return 0

    def start_lb(k, _):
        lb_copy(k).start()
        return 0

    def combine(msg, got):
        top = jnp.maximum(msg[0], jnp.max(got[:, 0], axis=0))
        tot = msg[1] * jnp.exp(msg[0] - top) + jnp.sum(
            got[:, 1] * jnp.exp(got[:, 0] - top[None]), axis=0
        )
        return top, tot, msg[2] + jnp.sum(got[:, 2], axis=0)

    lax.fori_loop(1, 16, start_la, 0)

    def wait_la(k, _):
        arrived(got_a.at[k - 1], la_r.at[k - 1])
        return 0

    lax.fori_loop(1, 16, wait_la, 0)
    top, tot, tlse = combine(msg_a, got_a)
    msg_b[0] = top
    msg_b[1] = tot
    msg_b[2] = tlse
    q2 = qual[...]
    qplane = jnp.where(row == 2 * t, jnp.broadcast_to(q2[0:1], (8, 128)), 0.0)
    msg_b[3] = jnp.where(row == 2 * t + 1, jnp.broadcast_to(q2[1:2], (8, 128)), qplane)
    lax.fori_loop(1, 16, start_lb, 0)

    def wait_lb(k, _):
        arrived(got_b.at[k - 1], lb_r.at[k - 1])
        return 0

    lax.fori_loop(1, 16, wait_lb, 0)
    top, tot, tlse = combine(msg_b, got_b)
    weight = (msg_b[3] + jnp.sum(got_b[:, 3], axis=0)) * (0.25 * LOSS_SCALE)
    planes[0] = weight * jnp.exp(msg_a[0] - top) / tot
    planes[1] = tlse - jnp.log(weight)

    def g_cross(b):
        at = (pl.ds(mult(b * BLK, BLK), BLK), pl.ds(mult(COLS * t, COLS), COLS))
        return remote(gs.at[at], gs.at[at], g_s.at[b, 0], g_r.at[b, 0], (cross, v))

    def g_sib(b):
        at = (pl.ds(mult(b * BLK, BLK), BLK), pl.ds(mult(COLS * t, COLS), COLS))
        return remote(gs.at[at], gs.at[at], g_s.at[b, 1], g_r.at[b, 1], (sib, v))

    def g_fwd(b):
        at = (pl.ds(mult(b * BLK, BLK), BLK), pl.ds(mult(COLS * cross, COLS), COLS))
        return remote(gs.at[at], gs.at[at], g_s.at[b, 2], g_r.at[b, 2], (sib, v))

    sub = lax.broadcasted_iota(jnp.int32, (16, 8, 128), 1) < 4

    def make_grads(b, _):
        rows = pl.ds(mult(b * BLK, BLK), BLK)
        for s in range(2):
            arrived(tb.at[2 * b + s], tb_r.at[2 * b + s])
        even = tb[pl.ds(mult(2 * b, 2), 2), :, 0].astype(F32).reshape(16, 16, 128)
        odd = tb[pl.ds(mult(2 * b, 2), 2), :, 1].astype(F32).reshape(16, 16, 128)
        scale = jnp.broadcast_to(planes[0, pl.ds(b, 1), :], (BLK, BLK)).T
        tl = jnp.broadcast_to(planes[1, pl.ds(b, 1), :], (BLK, BLK)).T
        for q in range(4):
            half = slice(8 * (q // 2), 8 * (q // 2) + 8)
            lo, hi = even[:, half], odd[:, half]
            if q % 2 == 0:
                mixed = jnp.where(sub, lo, pltpu.roll(hi, 4, 1))
            else:
                mixed = jnp.where(sub, pltpu.roll(lo, 4, 1), hi)
            teacher = mixed.reshape(BLK, 128)
            e = stu[rows, 128 * q : 128 * (q + 1)]
            g = e * scale - jnp.exp(teacher - tl)
            gs[rows, pl.ds(mult(COLS * t + 128 * q, 128), 128)] = g.astype(BF16)
        g_cross(b).start()
        g_sib(b).start()
        return 0

    lax.fori_loop(0, NB, make_grads, 0)
    c_head.wait()

    def line_peer(first, k):
        if first == 0:
            return (t, z * 16 + y * 4 + lax.rem(x + k, 4))
        return (t, z * 16 + lax.rem(y + k, 4) * 4 + x)

    def part1(b, par, k):
        if par == 0:
            return pb.at[b, :, lax.rem(x + k, 4)]
        return pb.at[b, lax.rem(y + k, 4)]

    def copy1(b, par, k):
        return remote(
            part1(b, par, k), r1.at[b, k - 1], r1_s.at[b, k - 1], r1_r.at[b, k - 1], line_peer(par, k)
        )

    def copy2(b, par, k):
        to = lax.rem(y + k, 4) if par == 0 else lax.rem(x + k, 4)
        return remote(
            s1.at[b, to], r2.at[b, k - 1], r2_s.at[b, k - 1], r2_r.at[b, k - 1], line_peer(1 - par, k)
        )

    def copy3(b):
        return remote(
            s2.at[b], fin.at[z, lax.rem(b, 2)], f_s.at[b], f_r.at[z, lax.rem(b, 2)], (b // 2, t * 16 + p)
        )

    def mine(b):
        return (b // 2 == t) & (t == z)

    def step1(b, par):
        rows = pl.ds(mult(b * BLK, BLK), BLK)
        arrived(gs.at[rows, pl.ds(mult(COLS * cross, COLS), COLS)], g_r.at[b, 0])
        g_fwd(b).start()
        arrived(gs.at[rows, pl.ds(mult(COLS * sib, COLS), COLS)], g_r.at[b, 1])
        arrived(gs.at[rows, pl.ds(mult(COLS * diag, COLS), COLS)], g_r.at[b, 2])
        part = lax.dot_general(
            headv[...], gs[rows, :], (((1,), (1,)), ((), ())), preferred_element_type=F32
        )
        pb[b] = part.reshape(4, 4, ROWS, BLK)
        for k in (2, 1, 3):
            copy1(b, par, k).start()

    def step2(b, par):
        for k in (1, 2, 3):
            arrived(r1.at[b, k - 1], r1_r.at[b, k - 1])
        own = pb[b, :, x] if par == 0 else pb[b, y]
        s1[b] = (own + r1[b, 0]) + (r1[b, 1] + r1[b, 2])
        for k in (2, 1, 3):
            copy2(b, par, k).start()

    def step3(b, par):
        for k in (1, 2, 3):
            arrived(r2.at[b, k - 1], r2_r.at[b, k - 1])
        own = s1[b, y] if par == 0 else s1[b, x]
        total = (own + r2[b, 0]) + (r2[b, 1] + r2[b, 2])
        s2[b] = total

        @pl.when(mine(b))
        def _():
            fin[z, lax.rem(b, 2)] = total

        @pl.when(jnp.logical_not(mine(b)))
        def _():
            copy3(b).start()

    def group_term(g, i):
        term = jnp.dot(
            hid_t[128 * i : 128 * (i + 1), pl.ds(mult(g * TG, TG), TG)],
            gs[pl.ds(mult(g * TG, TG), TG), :],
            preferred_element_type=F32,
        )
        return term.astype(BF16).astype(F32)

    def group(g, _):
        b0, b1 = 2 * g, 2 * g + 1
        step1(b0, 0)

        @pl.when(g > 0)
        def _():
            step2(b0 - 1, 1)
            step3(b0 - 2, 0)

        step1(b1, 1)
        step2(b0, 0)

        @pl.when(g > 0)
        def _():
            step3(b0 - 1, 1)

        @pl.when(g == 0)
        def _():
            for i in range(7):
                acc[128 * i : 128 * (i + 1), :] = group_term(g, i)

        @pl.when((g > 0) & (g < 3))
        def _():
            for i in range(7):
                acc[128 * i : 128 * (i + 1), :] += group_term(g, i)

        return 0

    lax.fori_loop(0, 4, group, 0)
    step2(7, 1)
    outs = []
    for i in range(7):
        rows = slice(128 * i, 128 * (i + 1))
        stage[rows, :] = (acc[rows, :] + group_term(3, i)).astype(BF16)
        cp = pltpu.make_async_copy(stage.at[pl.ds(128 * i, 128)], gh.at[pl.ds(128 * i, 128)], out_s.at[i])
        cp.start()
        outs.append(cp)
    step3(6, 0)
    step3(7, 1)

    for s in range(2):
        for k in range(4):

            @pl.when(jnp.logical_not((t == z) & (z == k)))
            def _():
                arrived(fin.at[k, s], f_r.at[k, s])

        hg[:, 128 * s : 128 * (s + 1)] = (
            (fin[0, s] + fin[1, s]) + (fin[2, s] + fin[3, s])
        ).astype(BF16)

    for cp in (h_cross, h_pair, h_sib, fwd1, fwd2):
        cp.wait_send()

    def drain(k, _):
        spread_copy(k).wait_send()
        ta_copy(k).wait_send()
        tb_copy(k).wait_send()
        la_copy(k).wait_send()
        lb_copy(k).wait_send()
        return 0

    lax.fori_loop(1, 16, drain, 0)

    def drain_blocks(g, _):
        for par in range(2):
            b = 2 * g + par
            g_cross(b).wait_send()
            g_sib(b).wait_send()
            g_fwd(b).wait_send()
            for k in (1, 2, 3):
                copy1(b, par, k).wait_send()
                copy2(b, par, k).wait_send()

            @pl.when(jnp.logical_not(mine(b)))
            def _():
                copy3(b).wait_send()

        return 0

    lax.fori_loop(0, 4, drain_blocks, 0)
    for cp in outs:
        cp.wait()


def body(hidden_states, student_head, teacher_logits, quality):
    teach = (
        teacher_logits.reshape(4, 256, 4, 128).transpose(1, 2, 0, 3).reshape(4, 16, 4, 16, 128)
    )
    any_ = pl.BlockSpec(memory_space=pl.ANY)
    vmem = pl.BlockSpec(memory_space=pltpu.VMEM)
    dma = pltpu.SemaphoreType.DMA
    hg, gh = pl.pallas_call(
        kernel,
        name="distill_backward",
        out_shape=(
            jax.ShapeDtypeStruct((ROWS, TG), BF16),
            jax.ShapeDtypeStruct((DS, 2048), BF16),
        ),
        in_specs=[any_, any_, any_, vmem],
        out_specs=(vmem, any_),
        scratch_shapes=[
            pltpu.VMEM((TOK, D), BF16),
            pltpu.VMEM((DS, 2048), BF16),
            pltpu.VMEM((4, DS, COLS), BF16),
            pltpu.VMEM((4, 16, 4, 16, 128), BF16),
            pltpu.VMEM((8, 2, 4, 4, 16, 128), BF16),
            pltpu.VMEM((16, 8, 2, 16, 128), BF16),
            pltpu.VMEM((TOK, COLS), F32),
            pltpu.VMEM((TOK, 2048), BF16),
            pltpu.VMEM((DS, TOK), BF16),
            pltpu.VMEM((DS, 2048), F32),
            pltpu.VMEM((DS, 2048), BF16),
            pltpu.VMEM((NB, 4, 4, ROWS, BLK), F32),
            pltpu.VMEM((NB, 3, 4, ROWS, BLK), F32),
            pltpu.VMEM((NB, 4, ROWS, BLK), F32),
            pltpu.VMEM((NB, 3, ROWS, BLK), F32),
            pltpu.VMEM((NB, ROWS, BLK), F32),
            pltpu.VMEM((4, 2, ROWS, BLK), F32),
            pltpu.VMEM((3, 8, 128), F32),
            pltpu.VMEM((15, 3, 8, 128), F32),
            pltpu.VMEM((4, 8, 128), F32),
            pltpu.VMEM((15, 4, 8, 128), F32),
            pltpu.VMEM((2, 8, 128), F32),
            dma((5,)),
            dma((4, 3)), dma((4, 4)),
            dma((5,)), dma((5,)),
            dma((15,)), dma((15,)),
            dma((15,)), dma((15,)),
            dma((16,)), dma((16,)),
            dma((15,)), dma((15,)),
            dma((15,)), dma((15,)),
            dma((NB, 3)), dma((NB, 3)),
            dma((NB, 3)), dma((NB, 3)),
            dma((NB, 3)), dma((NB, 3)),
            dma((NB,)), dma((4, 2)),
            dma((7,)),
        ],
        compiler_params=pltpu.CompilerParams(
            collective_id=0, has_side_effects=True, vmem_limit_bytes=60 * 2**20
        ),
        cost_estimate=pl.CostEstimate(
            flops=3 * 2 * TOK * DS * 2048, bytes_accessed=15 * 2**20, transcendentals=2**21
        ),
    )(hidden_states, student_head, teach, quality.reshape(2, 128))
    return hg.T, gh


def solution(mesh):
    return jax.shard_map(
        body,
        mesh=mesh,
        in_specs=(P("tok", None), P("tok", "voc"), P(("tok", "voc"), None), P("tok")),
        out_specs=(P("tok", "voc"), P("tok", "voc")),
        check_vma=False,
    )
```

```python
import functools

import jax
import jax.numpy as jnp
from jax import lax
from jax.experimental import pallas as pl
from jax.experimental.pallas import tpu as pltpu
from jax.sharding import PartitionSpec as P

MESH = pl.DeviceIdType.MESH
LOSS_SCALE = 64.0
D = 3584
DS = 896
TOK = 1024
TG = 256
COLS = 512
BLK = 128
TB_SPLIT = 8
NB = 8
ROWS = 56
CHUNKS = ((0, 256), (256, 256), (512, 256), (768, 128))
F32 = jnp.float32
BF16 = jnp.bfloat16


def mult(x, m):
    return pl.multiple_of(x, m)


def kernel(
    hid, head, teach, qual, hg, gh,
    hid_all, headv, hcols, tloc, ta, tb, stu, gs, hid_t, acc,
    pb, ax, ay, r1x, r1y, s1x, s1y, r2x, r2y, s2, fin,
    row_a, got_t, tq, st, got_a, row_b, got_b, full, scale,
    loc, head_s, head_r, hid_s, hid_r, bc_s, bc_r, ta_s, ta_r, tb_s, tb_r,
    t1_s, t1_r, t2_s, t2_r, la_s, la_r, lb_s, lb_r, lc_s, lc_r, g_s, g_r,
    ax_s, ax_r, ay_s, ay_r, r1x_s, r1x_r, r1y_s, r1y_r, r2x_s, r2x_r, r2y_s, r2y_r, f_s, f_r,
):
    t = lax.axis_index("tok")
    v = lax.axis_index("voc")
    z = v // 16
    p = v % 16
    y = p // 4
    x = p % 4
    c = t // 2
    h = t % 2
    sib = c * 2 + (1 - h)
    cross = (1 - c) * 2 + h
    diag = (1 - c) * 2 + (1 - h)
    tz = t * 4 + z

    def plane_peer(k):
        return (t, z * 16 + lax.rem(p + k, 16))

    def tz_peer(k):
        q = lax.rem(tz + k, 16)
        return (q // 4, (q % 4) * 16 + p)

    def remote(src, dst, ss, rs, dev):
        return pltpu.make_async_remote_copy(
            src_ref=src, dst_ref=dst, send_sem=ss, recv_sem=rs, device_id=dev, device_id_type=MESH
        )

    def arrived(ref, sem):
        pltpu.make_async_copy(ref, ref, sem).wait()

    bar = pltpu.get_barrier_semaphore()

    def greet(k, _):
        pl.semaphore_signal(bar, inc=1, device_id=plane_peer(k), device_id_type=MESH)
        pl.semaphore_signal(bar, inc=1, device_id=tz_peer(k), device_id_type=MESH)
        return 0

    lax.fori_loop(1, 16, greet, 0)

    c_own = pltpu.make_async_copy(head.at[:, pl.ds(mult(COLS * t, COLS), COLS)], hcols.at[t], loc.at[0])
    c_hid = pltpu.make_async_copy(hid, hid_all.at[pl.ds(mult(TG * t, TG), TG)], loc.at[1])
    order = (t, sib, cross, diag)
    c_heads = [
        pltpu.make_async_copy(
            head.at[:, pl.ds(mult(COLS * dev, COLS), COLS)], headv.at[:, pl.ds(COLS * j, COLS)], loc.at[5 + j]
        )
        for j, dev in enumerate(order)
    ]
    c_tl = pltpu.make_async_copy(teach, tloc, loc.at[3])
    c_ta = pltpu.make_async_copy(teach.at[:, p], ta.at[p // 2, p % 2], loc.at[4])
    for cp in (c_hid, c_own, c_tl, c_ta, *c_heads):
        cp.start()

    pl.semaphore_wait(bar, 30)

    def piece(group, q):
        return (
            pl.ds(mult(TG * group + 16 * (q // 2), 16), 16),
            pl.ds(mult(1792 * (q % 2), 128), 1792),
        )

    pr, pc = piece(0, p)
    mr, mc = piece(t, p)
    h_cross = remote(hid.at[pr, pc], hid_all.at[mr, mc], hid_s.at[0], hid_r.at[0], (cross, v))
    h_cross.start()
    znb = lax.rem(z + 2 * c + 3, 4)
    h_pair = remote(
        hid.at[pl.ds(128, 128)], hid_all.at[pl.ds(mult(TG * t + 128, 128), 128)],
        hid_s.at[1], hid_r.at[1], (cross, znb * 16 + p),
    )
    h_sib = remote(
        hid, hid_all.at[pl.ds(mult(TG * t, TG), TG)], hid_s.at[2], hid_r.at[2], (sib, v)
    )
    heads = []
    for i, (r0, rn) in enumerate(CHUNKS):
        for j, dev in enumerate((cross, diag, sib)):
            heads.append(
                remote(
                    head.at[pl.ds(r0, rn), pl.ds(mult(COLS * dev, COLS), COLS)],
                    hcols.at[t, pl.ds(r0, rn)],
                    head_s.at[i, j], head_r.at[t, i], (dev, v),
                )
            )
    for cp in heads[:3]:
        cp.start()
    h_pair.start()
    h_sib.start()
    for cp in heads[3:]:
        cp.start()

    xr, xc = piece(cross, p)
    arrived(hid_all.at[xr, xc], hid_r.at[0])

    def spread_copy(k):
        return remote(
            hid_all.at[xr, xc], hid_all.at[xr, xc], bc_s.at[k - 1], bc_r.at[k - 1], plane_peer(k)
        )

    def ta_copy(k):
        q = lax.rem(p + k, 16)
        return remote(
            teach.at[:, q], ta.at[p // 2, p % 2], ta_s.at[k - 1], ta_r.at[k - 1], plane_peer(k)
        )

    def start_spread(k, _):
        spread_copy(k).start()
        return 0

    def start_ta(k, _):
        ta_copy(k).start()
        return 0

    lax.fori_loop(1, 16, start_spread, 0)
    lax.fori_loop(1, 16, start_ta, 0)

    c_tl.wait()

    def tl_tile(i):
        return tloc[i // 4, pl.ds(mult((i % 4) * 4, 4), 4)].astype(F32)

    def top_step(i, m):
        return jnp.maximum(m, jnp.max(tl_tile(i), axis=(0, 1)))

    top16 = lax.fori_loop(0, 16, top_step, jnp.full((16, 128), -jnp.inf, F32))
    top16 = jnp.max(top16, axis=1, keepdims=True)
    top4 = jnp.maximum(jnp.maximum(top16[0:4], top16[4:8]), jnp.maximum(top16[8:12], top16[12:16]))
    top16 = jnp.concatenate([top4] * 4, axis=0)
    top_full = jnp.broadcast_to(top16, (16, 128))

    def sum_step(i, s):
        return s + jnp.sum(jnp.exp(tl_tile(i) - top_full), axis=(0, 1))

    sum16 = lax.fori_loop(0, 16, sum_step, jnp.zeros((16, 128), F32))
    sum16 = jnp.sum(sum16, axis=1, keepdims=True)
    sum4 = sum16[0:4] + sum16[4:8] + sum16[8:12] + sum16[12:16]
    lse4 = top4 + jnp.log(sum4)
    lane = lax.broadcasted_iota(jnp.int32, (1, 128), 1)
    low = lane < 64
    trow = jnp.zeros((1, 128), F32)
    for r in range(4):
        trow = jnp.where(lane == 4 * p + r, jnp.broadcast_to(lse4[r : r + 1], (1, 128)), trow)
    row_a[...] = trow

    def swap(a):
        return pltpu.roll(a, 64, len(a.shape) - 1)

    def t1_copy(k):
        return remote(row_a, got_t.at[k - 1], t1_s.at[k - 1], t1_r.at[k - 1], plane_peer(k))

    def t2_copy(k):
        return remote(tq.at[tz], tq.at[tz], t2_s.at[k - 1], t2_r.at[k - 1], tz_peer(k))

    def start_t1(k, _):
        t1_copy(k).start()
        return 0

    def start_t2(k, _):
        t2_copy(k).start()
        return 0

    lax.fori_loop(1, 16, start_t1, 0)

    def clear(i, _):
        acc[pl.ds(mult(i * 64, 64), 64), :] = jnp.zeros((64, 2048), F32)
        return 0

    lax.fori_loop(0, 14, clear, 0)

    def wait_t1(k, _):
        arrived(got_t.at[k - 1], t1_r.at[k - 1])
        return 0

    lax.fori_loop(1, 16, wait_t1, 0)
    tl_row = row_a[...] + jnp.sum(got_t[...], axis=0)
    q_row = qual[pl.ds(z // 2, 1), :]
    weight = LOSS_SCALE * jnp.where(lax.rem(z, 2) == 0, q_row, swap(q_row))
    tq[tz] = jnp.where(low, tl_row - jnp.log(weight), swap(weight))
    lax.fori_loop(1, 16, start_t2, 0)

    gx = mult(TG * cross, TG)

    def wait_spread(k, _):
        ar, ac = piece(cross, lax.rem(p + 16 - k, 16))
        arrived(hid_all.at[ar, ac], bc_r.at[k - 1])
        return 0

    lax.fori_loop(1, 16, wait_spread, 0)
    fwd1 = remote(
        hid_all.at[pl.ds(gx, 128)], hid_all.at[pl.ds(gx, 128)], hid_s.at[3], hid_r.at[3], (sib, v)
    )
    fwd1.start()
    gx2 = mult(TG * cross + 128, 128)
    arrived(hid_all.at[pl.ds(gx2, 128)], hid_r.at[1])
    fwd2 = remote(
        hid_all.at[pl.ds(gx2, 128)], hid_all.at[pl.ds(gx2, 128)], hid_s.at[4], hid_r.at[4], (sib, v)
    )
    fwd2.start()
    c_hid.wait()
    arrived(hid_all.at[pl.ds(mult(TG * sib, TG), TG)], hid_r.at[2])
    arrived(hid_all.at[pl.ds(mult(TG * diag, 128), 128)], hid_r.at[3])
    arrived(hid_all.at[pl.ds(mult(TG * diag + 128, 128), 128)], hid_r.at[4])

    def multiply(slot, r0, rn, first):
        base = mult(DS * slot + r0, 128)

        term = jnp.dot(
            hid_all[:, pl.ds(base, rn)], hcols[slot, pl.ds(r0, rn), :], preferred_element_type=F32
        )
        if first:
            stu[...] = term
        else:
            stu[...] += term

    def wait_head(slot, i):
        r0, rn = CHUNKS[i]
        arrived(hcols.at[slot, pl.ds(r0, rn)], head_r.at[slot, i])

    c_own.wait()
    multiply(t, 0, DS, True)
    for i in range(4):
        wait_head(sib, i)
    multiply(sib, 0, DS, False)

    def turn(i, _):
        rows = pl.ds(mult(i * 128, 128), 128)
        for j in range(7):
            block = hid_all[rows, pl.ds(mult(DS * t + 128 * j, 128), 128)]
            hid_t[128 * j : 128 * (j + 1), rows] = block.astype(F32).T.astype(BF16)
        return 0

    lax.fori_loop(0, 8, turn, 0)

    for i in range(3):
        r0, rn = CHUNKS[i]
        wait_head(cross, i)
        multiply(cross, r0, rn, False)
        wait_head(diag, i)
        multiply(diag, r0, rn, False)

    c_ta.wait()

    def wait_ta(k, _):
        q = lax.rem(p + 16 - k, 16)
        arrived(ta.at[q // 2, q % 2], ta_r.at[k - 1])
        return 0

    lax.fori_loop(1, 16, wait_ta, 0)
    wait_head(cross, 3)
    wait_head(diag, 3)
    for cp in heads:
        cp.wait_send()

    def tb_copy(k):
        q = lax.rem(tz + k, 16)
        return remote(
            ta.at[:, :, q % 4, q // 4], tb.at[tz], tb_s.at[k], tb_r.at[tz], tz_peer(k)
        )

    def start_tb(k, _):
        tb_copy(k).start()
        return 0

    lax.fori_loop(1, TB_SPLIT, start_tb, 0)
    c_tb = pltpu.make_async_copy(ta.at[:, :, z, t], tb.at[tz], tb_r.at[tz])
    c_tb.start()

    r0, rn = CHUNKS[3]
    multiply(cross, r0, rn, False)
    multiply(diag, r0, rn, False)

    def stats(b, _):
        rows = pl.ds(mult(b * BLK, BLK), BLK)
        val = stu[rows, :]
        top = jnp.max(val, axis=1, keepdims=True)
        e = jnp.exp(val - top)
        stu[rows, :] = e
        tot = jnp.sum(e, axis=1, keepdims=True)
        both = jnp.where(jnp.broadcast_to(low, (BLK, BLK)), top, tot).T
        m_row, s_row = both[0:1, :], both[64:65, :]
        st[2 * b] = jnp.where(low, m_row, swap(s_row))
        st[2 * b + 1] = jnp.where(low, swap(m_row), s_row)
        return 0

    lax.fori_loop(0, NB, stats, 0)

    def la_copy(k):
        return remote(
            st.at[lax.rem(p + k, 16)], got_a.at[k - 1], la_s.at[k - 1], la_r.at[k - 1], plane_peer(k)
        )

    def lb_copy(k):
        return remote(row_b, got_b.at[k - 1], lb_s.at[k - 1], lb_r.at[k - 1], tz_peer(k))

    def lc_copy(k):
        return remote(full.at[p], full.at[p], lc_s.at[k - 1], lc_r.at[k - 1], plane_peer(k))

    def start_la(k, _):
        la_copy(k).start()
        return 0

    def start_lb(k, _):
        lb_copy(k).start()
        return 0

    def start_lc(k, _):
        lc_copy(k).start()
        return 0

    def combine(mine, got):
        top = jnp.maximum(mine, jnp.max(got, axis=0))
        tot = swap(mine) * jnp.exp(mine - top) + jnp.sum(swap(got) * jnp.exp(got - top[None]), axis=0)
        return jnp.where(low, top, swap(tot))

    lax.fori_loop(1, 16, start_la, 0)

    def wait_la(k, _):
        arrived(got_a.at[k - 1], la_r.at[k - 1])
        return 0

    lax.fori_loop(1, 16, wait_la, 0)
    row_b[...] = combine(st[p], got_a[...])
    lax.fori_loop(1, 16, start_lb, 0)
    lax.fori_loop(TB_SPLIT, 16, start_tb, 0)

    def wait_lb(k, _):
        arrived(got_b.at[k - 1], lb_r.at[k - 1])
        return 0

    lax.fori_loop(1, 16, wait_lb, 0)
    full[p] = combine(row_b[...], got_b[...])
    lax.fori_loop(1, 16, start_lc, 0)

    def wait_t2(k, _):
        q = lax.rem(tz + 16 - k, 16)
        arrived(tq.at[q], t2_r.at[k - 1])
        return 0

    def wait_lc(k, _):
        q = lax.rem(p + 16 - k, 16)
        arrived(full.at[q], lc_r.at[k - 1])
        return 0

    lax.fori_loop(1, 16, wait_t2, 0)
    lax.fori_loop(1, 16, wait_lc, 0)
    scale[...] = swap(tq[...]) * jnp.exp(st[...] - full[...]) / swap(full[...])

    def g_copy(b, j, src, dst, dev):
        rows = pl.ds(mult(b * BLK, BLK), BLK)
        return remote(
            gs.at[rows, pl.ds(COLS * src, COLS)], gs.at[rows, pl.ds(COLS * dst, COLS)],
            g_s.at[b, j], g_r.at[b, j], (dev, v),
        )

    def g_cross(b):
        return g_copy(b, 0, 0, 2, cross)

    def g_sib(b):
        return g_copy(b, 1, 0, 1, sib)

    def g_fwd(b):
        return g_copy(b, 2, 2, 3, sib)

    def g_wait(b, j):
        slot = (2, 1, 3)[j]
        rows = pl.ds(mult(b * BLK, BLK), BLK)
        arrived(gs.at[rows, pl.ds(COLS * slot, COLS)], g_r.at[b, j])

    sub = lax.broadcasted_iota(jnp.int32, (16, 8, 128), 1) < 4

    def make_grads(b, _):
        rows = pl.ds(mult(b * BLK, BLK), BLK)
        for s in range(2):
            arrived(tb.at[2 * b + s], tb_r.at[2 * b + s])
        even = tb[pl.ds(mult(2 * b, 2), 2), :, 0].astype(F32).reshape(16, 16, 128)
        odd = tb[pl.ds(mult(2 * b, 2), 2), :, 1].astype(F32).reshape(16, 16, 128)
        sc_row = jnp.where(low, scale[2 * b], swap(scale[2 * b + 1]))
        tl_row = jnp.where(low, tq[2 * b], swap(tq[2 * b + 1]))
        sc = jnp.broadcast_to(sc_row, (BLK, BLK)).T
        tl = jnp.broadcast_to(tl_row, (BLK, BLK)).T
        for q in range(4):
            half = slice(8 * (q // 2), 8 * (q // 2) + 8)
            lo, hi = even[:, half], odd[:, half]
            if q % 2 == 0:
                mixed = jnp.where(sub, lo, pltpu.roll(hi, 4, 1))
            else:
                mixed = jnp.where(sub, pltpu.roll(lo, 4, 1), hi)
            teacher = mixed.reshape(BLK, 128)
            e = stu[rows, 128 * q : 128 * (q + 1)]
            g = e * sc - jnp.exp(teacher - tl)
            gs[rows, 128 * q : 128 * (q + 1)] = g.astype(BF16)
        g_cross(b).start()
        g_sib(b).start()
        return 0

    lax.fori_loop(0, NB, make_grads, 0)
    for cp in c_heads:
        cp.wait()

    ca = x + h * (y - x)
    cb = y + h * (x - y)

    def line_a(k):
        return (t, z * 16 + (1 - h) * (y * 4 + lax.rem(x + k, 4)) + h * (lax.rem(y + k, 4) * 4 + x))

    def line_b(k):
        return (t, z * 16 + h * (y * 4 + lax.rem(x + k, 4)) + (1 - h) * (lax.rem(y + k, 4) * 4 + x))

    def copies_a(b, i):
        k = 1 + 2 * i
        return (
            remote(
                pb.at[b, pl.ds(2 * i, 2), lax.rem(ca + 2, 4), pl.ds(0, 32)], ax.at[b, i],
                ax_s.at[b, i], ax_r.at[b, i], line_a(k),
            ),
            remote(
                pb.at[b, lax.rem(cb + 2, 4), pl.ds(2 * i, 2), pl.ds(32, 24)], ay.at[b, i],
                ay_s.at[b, i], ay_r.at[b, i], line_b(k),
            ),
        )

    def copies_b(b, i):
        k = 1 + 2 * i
        return (
            remote(
                pb.at[b, :, lax.rem(ca + k, 4), pl.ds(0, 32)], r1x.at[b, i],
                r1x_s.at[b, i], r1x_r.at[b, i], line_a(k),
            ),
            remote(
                pb.at[b, lax.rem(cb + k, 4), :, pl.ds(32, 24)], r1y.at[b, i],
                r1y_s.at[b, i], r1y_r.at[b, i], line_b(k),
            ),
        )

    def copies2(b, k):
        i = k - 1
        return (
            remote(
                s1x.at[b, lax.rem(cb + k, 4)], r2x.at[b, i], r2x_s.at[b, i], r2x_r.at[b, i], line_b(k)
            ),
            remote(
                s1y.at[b, lax.rem(ca + k, 4)], r2y.at[b, i], r2y_s.at[b, i], r2y_r.at[b, i], line_a(k)
            ),
        )

    def copy3(b):
        return remote(
            s2.at[b], fin.at[z, lax.rem(b, 2)], f_s.at[b], f_r.at[z, lax.rem(b, 2)], (b // 2, t * 16 + p)
        )

    def mine(b):
        return (b // 2 == t) & (t == z)

    def hand_on(b):
        g_wait(b, 0)
        g_fwd(b).start()

    def step1(b):
        rows = pl.ds(mult(b * BLK, BLK), BLK)
        g_wait(b, 1)
        g_wait(b, 2)
        out = lax.dot_general(
            headv[...], gs[rows, :], (((1,), (1,)), ((), ())), preferred_element_type=F32
        )
        for i in range(4):
            for j in range(4):
                first = ROWS * (4 * i + j)
                pb[b, i + h * (j - i), j + h * (i - j)] = out[first : first + ROWS]
        for i in range(2):
            for cp in copies_a(b, i):
                cp.start()

    def pass_on(b):
        for i in range(2):
            k = 1 + 2 * i
            to_a, to_b = lax.rem(ca + k, 4), lax.rem(cb + k, 4)
            arrived(ax.at[b, i], ax_r.at[b, i])
            pb[b, 2 * i : 2 * i + 2, to_a, 0:32] += ax[b, i]
            arrived(ay.at[b, i], ay_r.at[b, i])
            pb[b, to_b, 2 * i : 2 * i + 2, 32:56] += ay[b, i]
            for cp in copies_b(b, i):
                cp.start()

    def step2(b):
        for i in range(2):
            arrived(r1x.at[b, i], r1x_r.at[b, i])
            arrived(r1y.at[b, i], r1y_r.at[b, i])
        s1x[b] = pb[b, :, ca, 0:32] + r1x[b, 0] + r1x[b, 1]
        s1y[b] = pb[b, cb, :, 32:56] + r1y[b, 0] + r1y[b, 1]
        for k in (2, 1, 3):
            for cp in copies2(b, k):
                cp.start()

    def step3(b):
        for k in (1, 2, 3):
            arrived(r2x.at[b, k - 1], r2x_r.at[b, k - 1])
            arrived(r2y.at[b, k - 1], r2y_r.at[b, k - 1])
        s2[b, 0:32] = (s1x[b, cb] + r2x[b, 0]) + (r2x[b, 1] + r2x[b, 2])
        s2[b, 32:56] = (s1y[b, ca] + r2y[b, 0]) + (r2y[b, 1] + r2y[b, 2])

        @pl.when(mine(b))
        def _():
            fin[z, lax.rem(b, 2)] = s2[b]

        @pl.when(jnp.logical_not(mine(b)))
        def _():
            copy3(b).start()

    def group_term(g, i, half):
        term = jnp.dot(
            hid_t[128 * i : 128 * (i + 1), pl.ds(mult(g * TG, TG), TG)],
            gs[pl.ds(mult(g * TG, TG), TG), 1024 * half : 1024 * (half + 1)],
            preferred_element_type=F32,
        )
        return term.astype(BF16).astype(F32)

    def add_group(g, half):
        for i in range(7):
            rows = slice(128 * i, 128 * (i + 1))
            cols = slice(1024 * half, 1024 * (half + 1))
            new = acc[rows, cols] + group_term(g, i, half)
            acc[rows, cols] = new
            out = new.astype(BF16)
            for j in range(2):
                at = mult(COLS * order[2 * half + j], COLS)
                gh[rows, pl.ds(at, COLS)] = out[:, COLS * j : COLS * (j + 1)]

    hand_on(0)
    hand_on(1)

    def when(condition, step, *args):
        @pl.when(condition)
        def _():
            step(*args)

    def block(i, _):
        odd = lax.rem(i, 2) == 1
        when(i < 8, step1, i)
        when(i < 6, hand_on, i + 2)
        when((i > 0) & (i < 9), pass_on, i - 1)
        when(odd & (i < 8), add_group, i // 2, 0)
        when(jnp.logical_not(odd) & (i > 0) & (i < 9), add_group, i // 2 - 1, 1)
        when((i > 1) & (i < 10), step2, i - 2)
        when(i > 3, step3, i - 4)
        return 0

    lax.fori_loop(0, 12, block, 0)

    for s in range(2):
        for k in range(4):

            @pl.when(jnp.logical_not((t == z) & (z == k)))
            def _():
                arrived(fin.at[k, s], f_r.at[k, s])

        hg[:, 128 * s : 128 * (s + 1)] = (
            (fin[0, s] + fin[1, s]) + (fin[2, s] + fin[3, s])
        ).astype(BF16)

    for cp in (h_cross, h_pair, h_sib, fwd1, fwd2):
        cp.wait_send()

    def drain(k, _):
        spread_copy(k).wait_send()
        ta_copy(k).wait_send()
        tb_copy(k).wait_send()
        t1_copy(k).wait_send()
        t2_copy(k).wait_send()
        la_copy(k).wait_send()
        lb_copy(k).wait_send()
        lc_copy(k).wait_send()
        return 0

    lax.fori_loop(1, 16, drain, 0)

    def drain_blocks(b, _):
        g_cross(b).wait_send()
        g_sib(b).wait_send()
        g_fwd(b).wait_send()
        for i in range(2):
            for cp in copies_a(b, i) + copies_b(b, i):
                cp.wait_send()
        for k in (1, 2, 3):
            for cp in copies2(b, k):
                cp.wait_send()

        @pl.when(jnp.logical_not(mine(b)))
        def _():
            copy3(b).wait_send()

        return 0

    lax.fori_loop(0, NB, drain_blocks, 0)


def hand_over(hg_in, gh_in, hg, gh, sem):
    a = pltpu.make_async_copy(hg_in, hg, sem.at[0])
    b = pltpu.make_async_copy(gh_in, gh, sem.at[1])
    a.start()
    b.start()
    a.wait()
    b.wait()


def body(hidden_states, student_head, teacher_logits, quality):
    teach = (
        teacher_logits.reshape(4, 256, 4, 128).transpose(1, 2, 0, 3).reshape(4, 16, 4, 16, 128)
    )
    hbm = pl.BlockSpec(memory_space=pltpu.HBM)
    vmem = pl.BlockSpec(memory_space=pltpu.VMEM)
    dma = pltpu.SemaphoreType.DMA
    hg, gh = pl.pallas_call(
        kernel,
        name="distill_backward",
        out_shape=(pltpu.VMEM((ROWS, TG), BF16), pltpu.VMEM((DS, 2048), BF16)),
        in_specs=[hbm, hbm, hbm, vmem],
        out_specs=(vmem, vmem),
        scratch_shapes=[
            pltpu.VMEM((TOK, D), BF16),
            pltpu.VMEM((DS, 2048), BF16),
            pltpu.VMEM((4, DS, COLS), BF16),
            pltpu.VMEM((4, 16, 4, 16, 128), BF16),
            pltpu.VMEM((8, 2, 4, 4, 16, 128), BF16),
            pltpu.VMEM((16, 8, 2, 16, 128), BF16),
            pltpu.VMEM((TOK, COLS), F32),
            pltpu.VMEM((TOK, 2048), BF16),
            pltpu.VMEM((DS, TOK), BF16),
            pltpu.VMEM((DS, 2048), F32),
            pltpu.VMEM((NB, 4, 4, ROWS, BLK), F32),
            pltpu.VMEM((NB, 2, 2, 32, BLK), F32),
            pltpu.VMEM((NB, 2, 2, 24, BLK), F32),
            pltpu.VMEM((NB, 2, 4, 32, BLK), F32),
            pltpu.VMEM((NB, 2, 4, 24, BLK), F32),
            pltpu.VMEM((NB, 4, 32, BLK), F32),
            pltpu.VMEM((NB, 4, 24, BLK), F32),
            pltpu.VMEM((NB, 3, 32, BLK), F32),
            pltpu.VMEM((NB, 3, 24, BLK), F32),
            pltpu.VMEM((NB, ROWS, BLK), F32),
            pltpu.VMEM((4, 2, ROWS, BLK), F32),
            pltpu.VMEM((1, 128), F32),
            pltpu.VMEM((15, 1, 128), F32),
            pltpu.VMEM((16, 1, 128), F32),
            pltpu.VMEM((16, 1, 128), F32),
            pltpu.VMEM((15, 1, 128), F32),
            pltpu.VMEM((1, 128), F32),
            pltpu.VMEM((15, 1, 128), F32),
            pltpu.VMEM((16, 1, 128), F32),
            pltpu.VMEM((16, 1, 128), F32),
            dma((9,)),
            dma((4, 3)), dma((4, 4)),
            dma((5,)), dma((5,)),
            dma((15,)), dma((15,)),
            dma((15,)), dma((15,)),
            dma((16,)), dma((16,)),
            dma((15,)), dma((15,)),
            dma((15,)), dma((15,)),
            dma((15,)), dma((15,)),
            dma((15,)), dma((15,)),
            dma((15,)), dma((15,)),
            dma((NB, 3)), dma((NB, 3)),
            dma((NB, 2)), dma((NB, 2)),
            dma((NB, 2)), dma((NB, 2)),
            dma((NB, 2)), dma((NB, 2)),
            dma((NB, 2)), dma((NB, 2)),
            dma((NB, 3)), dma((NB, 3)),
            dma((NB, 3)), dma((NB, 3)),
            dma((NB,)), dma((4, 2)),
        ],
        compiler_params=pltpu.CompilerParams(
            collective_id=0, has_side_effects=True, vmem_limit_bytes=55 * 2**20
        ),
        cost_estimate=pl.CostEstimate(
            flops=3 * 2 * TOK * DS * 2048, bytes_accessed=15 * 2**20, transcendentals=2**21
        ),
    )(hidden_states, student_head, teach, quality.reshape(2, 128))
    hg, gh = pl.pallas_call(
        hand_over,
        name="results",
        out_shape=(
            jax.ShapeDtypeStruct((ROWS, TG), BF16),
            jax.ShapeDtypeStruct((DS, 2048), BF16),
        ),
        in_specs=[vmem, vmem],
        out_specs=(hbm, hbm),
        scratch_shapes=[dma((2,))],
        compiler_params=pltpu.CompilerParams(vmem_limit_bytes=2**20),
    )(
        pltpu.with_memory_space_constraint(hg, pltpu.VMEM),
        pltpu.with_memory_space_constraint(gh, pltpu.VMEM),
    )
    return hg.T, gh


def solution(mesh):
    return jax.shard_map(
        body,
        mesh=mesh,
        in_specs=(P("tok", None), P("tok", "voc"), P(("tok", "voc"), None), P("tok")),
        out_specs=(P("tok", "voc"), P("tok", "voc")),
        check_vma=False,
    )
```

```python
import functools

import jax
import jax.numpy as jnp
from jax import lax
from jax.experimental import pallas as pl
from jax.experimental.pallas import tpu as pltpu
from jax.sharding import PartitionSpec as P

MESH = pl.DeviceIdType.MESH
LOSS_SCALE = 64.0
D = 3584
DS = 896
TOK = 1024
TG = 256
COLS = 512
BLK = 128
TB_SPLIT = 8
NB = 8
NX = 3
NS = NB + NX
ROWS = 56
CHUNKS = ((0, 256), (256, 256), (512, 256), (768, 128))
F32 = jnp.float32
BF16 = jnp.bfloat16


def mult(x, m):
    return pl.multiple_of(x, m)


def kernel(
    hid, head, teach, qual, hg, gh,
    hid_all, headv, hcols, hxc, tloc, ta, tb, stu, gs, hid_t, acc,
    pb, zx, zy, r1x, r1y, s1x, s1y, z2x, z2y, r2x, r2y, s2, fin,
    row_a, got_t, tq, st, got_a, row_b, got_b, full, scale,
    loc, head_s, head_r, hx_s, hx_r, hid_s, hid_r, bc_s, bc_r, ta_s, ta_r, tb_s, tb_r,
    t1_s, t1_r, t2_s, t2_r, la_s, la_r, lb_s, lb_r, lc_s, lc_r, g_s, g_r,
    r1x_s, r1x_r, r1y_s, r1y_r, r2x_s, r2x_r, r2y_s, r2y_r, f_s, f_r,
):
    t = lax.axis_index("tok")
    v = lax.axis_index("voc")
    z = v // 16
    p = v % 16
    y = p // 4
    x = p % 4
    c = t // 2
    h = t % 2
    sib = c * 2 + (1 - h)
    cross = (1 - c) * 2 + h
    diag = (1 - c) * 2 + (1 - h)
    tz = t * 4 + z

    def plane_peer(k):
        return (t, z * 16 + lax.rem(p + k, 16))

    def tz_peer(k):
        q = lax.rem(tz + k, 16)
        return (q // 4, (q % 4) * 16 + p)

    def remote(src, dst, ss, rs, dev):
        return pltpu.make_async_remote_copy(
            src_ref=src, dst_ref=dst, send_sem=ss, recv_sem=rs, device_id=dev, device_id_type=MESH
        )

    def arrived(ref, sem):
        pltpu.make_async_copy(ref, ref, sem).wait()

    bar = pltpu.get_barrier_semaphore()

    def greet(k, _):
        pl.semaphore_signal(bar, inc=1, device_id=plane_peer(k), device_id_type=MESH)
        pl.semaphore_signal(bar, inc=1, device_id=tz_peer(k), device_id_type=MESH)
        return 0

    lax.fori_loop(1, 16, greet, 0)

    c_own = pltpu.make_async_copy(head.at[:, pl.ds(mult(COLS * t, COLS), COLS)], hcols.at[t], loc.at[0])
    c_hid = pltpu.make_async_copy(hid, hid_all.at[pl.ds(mult(TG * t, TG), TG)], loc.at[1])
    order = (t, sib, cross, diag)
    c_heads = [
        pltpu.make_async_copy(
            head.at[:, pl.ds(mult(COLS * dev, COLS), COLS)], headv.at[:, pl.ds(COLS * j, COLS)], loc.at[5 + j]
        )
        for j, dev in enumerate(order)
    ]
    c_tl = pltpu.make_async_copy(teach, tloc, loc.at[3])
    c_ta = pltpu.make_async_copy(teach.at[:, p], ta.at[p // 2, p % 2], loc.at[4])
    for cp in (c_hid, c_own, c_tl, c_ta, *c_heads):
        cp.start()

    pl.semaphore_wait(bar, 30)

    def piece(group, q):
        return (
            pl.ds(mult(TG * group + 16 * (q // 2), 16), 16),
            pl.ds(mult(1792 * (q % 2), 128), 1792),
        )

    pr, pc = piece(0, p)
    mr, mc = piece(t, p)
    znb = lax.rem(z + 2 * c + 3, 4)
    h_cross = remote(
        hid.at[pr, pc], hid_all.at[mr, mc], hid_s.at[0], hid_r.at[0], (cross, znb * 16 + p)
    )
    h_cross.start()
    h_pair = remote(
        hid.at[pl.ds(128, 128)], hid_all.at[pl.ds(mult(TG * t + 128, 128), 128)],
        hid_s.at[1], hid_r.at[1], (cross, znb * 16 + p),
    )
    h_sib = remote(
        hid, hid_all.at[pl.ds(mult(TG * t, TG), TG)], hid_s.at[2], hid_r.at[2], (sib, v)
    )
    heads = []
    for i, (r0, rn) in enumerate(CHUNKS):
        for j, dev in enumerate((cross, diag, sib)):
            heads.append(
                remote(
                    head.at[pl.ds(r0, rn), pl.ds(mult(COLS * dev, COLS), COLS)],
                    hcols.at[t, pl.ds(r0, rn)],
                    head_s.at[i, j], head_r.at[t, i], (dev, v),
                )
            )
    for cp in heads[:3]:
        cp.start()
    h_pair.start()
    h_sib.start()
    for cp in heads[3:]:
        cp.start()

    xr, xc = piece(cross, p)
    arrived(hid_all.at[xr, xc], hid_r.at[0])

    def spread_copy(k):
        return remote(
            hid_all.at[xr, xc], hid_all.at[xr, xc], bc_s.at[k - 1], bc_r.at[k - 1], plane_peer(k)
        )

    def ta_copy(k):
        q = lax.rem(p + k, 16)
        return remote(
            teach.at[:, q], ta.at[p // 2, p % 2], ta_s.at[k - 1], ta_r.at[k - 1], plane_peer(k)
        )

    def start_spread(k, _):
        spread_copy(k).start()
        return 0

    def start_ta(k, _):
        ta_copy(k).start()
        return 0

    lax.fori_loop(1, 16, start_spread, 0)
    lax.fori_loop(1, 16, start_ta, 0)

    c_tl.wait()

    def tl_tile(i):
        return tloc[i // 4, pl.ds(mult((i % 4) * 4, 4), 4)].astype(F32)

    def top_step(i, m):
        return jnp.maximum(m, jnp.max(tl_tile(i), axis=(0, 1)))

    top16 = lax.fori_loop(0, 16, top_step, jnp.full((16, 128), -jnp.inf, F32))
    top16 = jnp.max(top16, axis=1, keepdims=True)
    top4 = jnp.maximum(jnp.maximum(top16[0:4], top16[4:8]), jnp.maximum(top16[8:12], top16[12:16]))
    top16 = jnp.concatenate([top4] * 4, axis=0)
    top_full = jnp.broadcast_to(top16, (16, 128))

    def sum_step(i, s):
        return s + jnp.sum(jnp.exp(tl_tile(i) - top_full), axis=(0, 1))

    sum16 = lax.fori_loop(0, 16, sum_step, jnp.zeros((16, 128), F32))
    sum16 = jnp.sum(sum16, axis=1, keepdims=True)
    sum4 = sum16[0:4] + sum16[4:8] + sum16[8:12] + sum16[12:16]
    lse4 = top4 + jnp.log(sum4)
    lane = lax.broadcasted_iota(jnp.int32, (1, 128), 1)
    low = lane < 64
    trow = jnp.zeros((1, 128), F32)
    for r in range(4):
        trow = jnp.where(lane == 4 * p + r, jnp.broadcast_to(lse4[r : r + 1], (1, 128)), trow)
    row_a[...] = trow

    def swap(a):
        return pltpu.roll(a, 64, len(a.shape) - 1)

    def t1_copy(k):
        return remote(row_a, got_t.at[k - 1], t1_s.at[k - 1], t1_r.at[k - 1], plane_peer(k))

    def t2_copy(k):
        return remote(tq.at[tz], tq.at[tz], t2_s.at[k - 1], t2_r.at[k - 1], tz_peer(k))

    def start_t1(k, _):
        t1_copy(k).start()
        return 0

    def start_t2(k, _):
        t2_copy(k).start()
        return 0

    lax.fori_loop(1, 16, start_t1, 0)

    def clear(i, _):
        acc[pl.ds(mult(i * 64, 64), 64), :] = jnp.zeros((64, 2048), F32)
        return 0

    lax.fori_loop(0, 14, clear, 0)

    def wait_t1(k, _):
        arrived(got_t.at[k - 1], t1_r.at[k - 1])
        return 0

    lax.fori_loop(1, 16, wait_t1, 0)
    tl_row = row_a[...] + jnp.sum(got_t[...], axis=0)
    q_row = qual[pl.ds(z // 2, 1), :]
    weight = LOSS_SCALE * jnp.where(lax.rem(z, 2) == 0, q_row, swap(q_row))
    tq[tz] = jnp.where(low, tl_row - jnp.log(weight), swap(weight))
    lax.fori_loop(1, 16, start_t2, 0)

    gx = mult(TG * cross, TG)

    def wait_spread(k, _):
        ar, ac = piece(cross, lax.rem(p + 16 - k, 16))
        arrived(hid_all.at[ar, ac], bc_r.at[k - 1])
        return 0

    lax.fori_loop(1, 16, wait_spread, 0)
    fwd1 = remote(
        hid_all.at[pl.ds(gx, 128)], hid_all.at[pl.ds(gx, 128)], hid_s.at[3], hid_r.at[3], (sib, v)
    )
    fwd1.start()
    gx2 = mult(TG * cross + 128, 128)
    arrived(hid_all.at[pl.ds(gx2, 128)], hid_r.at[1])
    fwd2 = remote(
        hid_all.at[pl.ds(gx2, 128)], hid_all.at[pl.ds(gx2, 128)], hid_s.at[4], hid_r.at[4], (sib, v)
    )
    fwd2.start()
    c_hid.wait()
    arrived(hid_all.at[pl.ds(mult(TG * sib, TG), TG)], hid_r.at[2])
    arrived(hid_all.at[pl.ds(mult(TG * diag, 128), 128)], hid_r.at[3])
    arrived(hid_all.at[pl.ds(mult(TG * diag + 128, 128), 128)], hid_r.at[4])

    def multiply(slot, r0, rn, first):
        base = mult(DS * slot + r0, 128)

        term = jnp.dot(
            hid_all[:, pl.ds(base, rn)], hcols[slot, pl.ds(r0, rn), :], preferred_element_type=F32
        )
        if first:
            stu[...] = term
        else:
            stu[...] += term

    def wait_head(slot, i):
        r0, rn = CHUNKS[i]
        arrived(hcols.at[slot, pl.ds(r0, rn)], head_r.at[slot, i])

    c_own.wait()
    multiply(t, 0, DS, True)
    for i in range(4):
        wait_head(sib, i)
    multiply(sib, 0, DS, False)

    def turn(i, _):
        rows = pl.ds(mult(i * 128, 128), 128)
        for j in range(7):
            block = hid_all[rows, pl.ds(mult(DS * t + 128 * j, 128), 128)]
            hid_t[128 * j : 128 * (j + 1), rows] = block.astype(F32).T.astype(BF16)
        return 0

    lax.fori_loop(0, 8, turn, 0)

    for i in range(3):
        r0, rn = CHUNKS[i]
        wait_head(cross, i)
        multiply(cross, r0, rn, False)
        wait_head(diag, i)
        multiply(diag, r0, rn, False)

    c_ta.wait()

    def wait_ta(k, _):
        q = lax.rem(p + 16 - k, 16)
        arrived(ta.at[q // 2, q % 2], ta_r.at[k - 1])
        return 0

    lax.fori_loop(1, 16, wait_ta, 0)
    def tb_copy(k):
        q = lax.rem(tz + k, 16)
        return remote(
            ta.at[:, :, q % 4, q // 4], tb.at[tz], tb_s.at[k], tb_r.at[tz], tz_peer(k)
        )

    def is_early(k):
        q = lax.rem(tz + k, 16)
        t2, zq = q // 4, q % 4
        return ((t2 // 2 != c) & (zq == znb)) | ((t2 == sib) & (zq == z))

    def start_tb(k, _):
        @pl.when(jnp.logical_not(is_early(k)))
        def _():
            tb_copy(k).start()

        return 0

    def start_early(k, _):
        @pl.when(is_early(k))
        def _():
            tb_copy(k).start()

        return 0

    lax.fori_loop(1, 16, start_early, 0)
    wait_head(cross, 3)
    wait_head(diag, 3)
    for cp in heads:
        cp.wait_send()
    lax.fori_loop(1, TB_SPLIT, start_tb, 0)
    c_tb = pltpu.make_async_copy(ta.at[:, :, z, t], tb.at[tz], tb_r.at[tz])
    c_tb.start()

    c_hx = pltpu.make_async_copy(hcols.at[cross], hxc.at[:, pl.ds(0, COLS)], loc.at[9])
    c_hx.start()
    h_hx = remote(hcols.at[diag], hxc.at[:, pl.ds(COLS, COLS)], hx_s.at[0], hx_r.at[0], (sib, v))
    h_hx.start()

    r0, rn = CHUNKS[3]
    multiply(cross, r0, rn, False)
    multiply(diag, r0, rn, False)

    def stats(b, _):
        rows = pl.ds(mult(b * BLK, BLK), BLK)
        val = stu[rows, :]
        top = jnp.max(val, axis=1, keepdims=True)
        e = jnp.exp(val - top)
        stu[rows, :] = e
        tot = jnp.sum(e, axis=1, keepdims=True)
        both = jnp.where(jnp.broadcast_to(low, (BLK, BLK)), top, tot).T
        m_row, s_row = both[0:1, :], both[64:65, :]
        st[2 * b] = jnp.where(low, m_row, swap(s_row))
        st[2 * b + 1] = jnp.where(low, swap(m_row), s_row)
        return 0

    lax.fori_loop(0, NB, stats, 0)

    def la_copy(k):
        return remote(
            st.at[lax.rem(p + k, 16)], got_a.at[k - 1], la_s.at[k - 1], la_r.at[k - 1], plane_peer(k)
        )

    def lb_copy(k):
        return remote(row_b, got_b.at[k - 1], lb_s.at[k - 1], lb_r.at[k - 1], tz_peer(k))

    def lc_copy(k):
        return remote(full.at[p], full.at[p], lc_s.at[k - 1], lc_r.at[k - 1], plane_peer(k))

    def start_la(k, _):
        la_copy(k).start()
        return 0

    def start_lb(k, _):
        lb_copy(k).start()
        return 0

    def start_lc(k, _):
        lc_copy(k).start()
        return 0

    def combine(mine, got):
        top = jnp.maximum(mine, jnp.max(got, axis=0))
        tot = swap(mine) * jnp.exp(mine - top) + jnp.sum(swap(got) * jnp.exp(got - top[None]), axis=0)
        return jnp.where(low, top, swap(tot))

    lax.fori_loop(1, 16, start_la, 0)

    def wait_la(k, _):
        arrived(got_a.at[k - 1], la_r.at[k - 1])
        return 0

    lax.fori_loop(1, 16, wait_la, 0)
    row_b[...] = combine(st[p], got_a[...])
    lax.fori_loop(1, 16, start_lb, 0)
    lax.fori_loop(TB_SPLIT, 16, start_tb, 0)

    def wait_lb(k, _):
        arrived(got_b.at[k - 1], lb_r.at[k - 1])
        return 0

    lax.fori_loop(1, 16, wait_lb, 0)
    full[p] = combine(row_b[...], got_b[...])
    lax.fori_loop(1, 16, start_lc, 0)

    def wait_t2(k, _):
        q = lax.rem(tz + 16 - k, 16)
        arrived(tq.at[q], t2_r.at[k - 1])
        return 0

    def wait_lc(k, _):
        q = lax.rem(p + 16 - k, 16)
        arrived(full.at[q], lc_r.at[k - 1])
        return 0

    lax.fori_loop(1, 16, wait_t2, 0)
    lax.fori_loop(1, 16, wait_lc, 0)
    scale[...] = swap(tq[...]) * jnp.exp(st[...] - full[...]) / swap(full[...])

    def g_copy(b, j, src, dst, dev):
        rows = pl.ds(mult(b * BLK, BLK), BLK)
        return remote(
            gs.at[rows, pl.ds(COLS * src, COLS)], gs.at[rows, pl.ds(COLS * dst, COLS)],
            g_s.at[b, j], g_r.at[b, j], (dev, v),
        )

    def g_cross(b):
        return g_copy(b, 0, 0, 2, cross)

    def g_sib(b):
        return g_copy(b, 1, 0, 1, sib)

    def g_fwd(b):
        return g_copy(b, 2, 2, 3, sib)

    def g_wait(b, j):
        slot = (2, 1, 3)[j]
        rows = pl.ds(mult(b * BLK, BLK), BLK)
        arrived(gs.at[rows, pl.ds(COLS * slot, COLS)], g_r.at[b, j])

    sub = lax.broadcasted_iota(jnp.int32, (16, 8, 128), 1) < 4

    def make_grads(b, _):
        rows = pl.ds(mult(b * BLK, BLK), BLK)
        for s in range(2):
            arrived(tb.at[2 * b + s], tb_r.at[2 * b + s])
        even = tb[pl.ds(mult(2 * b, 2), 2), :, 0].astype(F32).reshape(16, 16, 128)
        odd = tb[pl.ds(mult(2 * b, 2), 2), :, 1].astype(F32).reshape(16, 16, 128)
        sc_row = jnp.where(low, scale[2 * b], swap(scale[2 * b + 1]))
        tl_row = jnp.where(low, tq[2 * b], swap(tq[2 * b + 1]))
        sc = jnp.broadcast_to(sc_row, (BLK, BLK)).T
        tl = jnp.broadcast_to(tl_row, (BLK, BLK)).T
        for q in range(4):
            half = slice(8 * (q // 2), 8 * (q // 2) + 8)
            lo, hi = even[:, half], odd[:, half]
            if q % 2 == 0:
                mixed = jnp.where(sub, lo, pltpu.roll(hi, 4, 1))
            else:
                mixed = jnp.where(sub, pltpu.roll(lo, 4, 1), hi)
            teacher = mixed.reshape(BLK, 128)
            e = stu[rows, 128 * q : 128 * (q + 1)]
            g = e * sc - jnp.exp(teacher - tl)
            gs[rows, 128 * q : 128 * (q + 1)] = g.astype(BF16)
        g_sib(b).start()

        @pl.when(b < NB - NX)
        def _():
            g_cross(b).start()

        return 0

    lax.fori_loop(0, NB, make_grads, 0)
    for b in range(NB - NX, NB):
        g_cross(b).start()
    c_hx.wait()
    arrived(hxc.at[:, pl.ds(COLS, COLS)], hx_r.at[0])
    for cp in c_heads:
        cp.wait()

    ca = x + h * (y - x)
    cb = y + h * (x - y)

    def line_a(k):
        return (t, z * 16 + (1 - h) * (y * 4 + lax.rem(x + k, 4)) + h * (lax.rem(y + k, 4) * 4 + x))

    def line_b(k):
        return (t, z * 16 + h * (y * 4 + lax.rem(x + k, 4)) + (1 - h) * (lax.rem(y + k, 4) * 4 + x))

    def copies1(b, k):
        i = k - 1
        return (
            remote(zx.at[b, i], r1x.at[b, i], r1x_s.at[b, i], r1x_r.at[b, i], line_a(k)),
            remote(zy.at[b, i], r1y.at[b, i], r1y_s.at[b, i], r1y_r.at[b, i], line_b(k)),
        )

    def copies2(b, k):
        i = k - 1
        return (
            remote(z2x.at[b, i], r2x.at[b, i], r2x_s.at[b, i], r2x_r.at[b, i], line_b(k)),
            remote(z2y.at[b, i], r2y.at[b, i], r2y_s.at[b, i], r2y_r.at[b, i], line_a(k)),
        )

    def block_of(n):
        return n - NX * (n // NB)

    def run_of(n):
        return t + (n // NB) * (cross - t)

    def copy3(n):
        b = block_of(n)
        at = (n // NB, z, lax.rem(b, 2))
        return remote(s2.at[n], fin.at[at], f_s.at[n], f_r.at[at], (b // 2, run_of(n) * 16 + p))

    def mine(n):
        return (block_of(n) // 2 == t) & (run_of(n) == z)

    def hand_on(b):
        g_wait(b, 0)
        g_fwd(b).start()

    def dot_t(a, b):
        return lax.dot_general(a, b, (((1,), (1,)), ((), ())), preferred_element_type=F32)

    def step1(b):
        rows = pl.ds(mult(b * BLK, BLK), BLK)
        g_wait(b, 1)
        g_wait(b, 2)
        keep(b, dot_t(headv[...], gs[rows, :]), 0)
        spread(b)

    def alone_blocks():
        for b in range(NB - NX, NB):
            g_wait(b, 1)
        for n, rows_of in ((NB - NX, headv), (NB, hxc)):
            for m in range(2):
                out = dot_t(
                    rows_of[448 * m : 448 * (m + 1), 0 : 2 * COLS],
                    gs[BLK * (NB - NX) :, 0 : 2 * COLS],
                )
                for k in range(NX):
                    keep(n + k, out[:, BLK * k : BLK * (k + 1)], 2 * m)
        for k in range(NX):
            spread(NB - NX + k)
            spread(NB + k)

    def keep(n, out, begin):
        for i in range(begin, begin + out.shape[0] // (4 * ROWS)):
            for j in range(4):
                first = ROWS * (4 * (i - begin) + j)
                pb[n, i + h * (j - i), j + h * (i - j)] = out[first : first + ROWS]

    def spread(b):
        for k in (2, 1, 3):
            to_a, to_b = lax.rem(ca + k, 4), lax.rem(cb + k, 4)
            zx[b, k - 1] = pb[b, :, to_a, 0:32].reshape(128, BLK).astype(BF16)
            zy[b, k - 1] = pb[b, to_b, :, 32:56].reshape(96, BLK).astype(BF16)
            for cp in copies1(b, k):
                cp.start()

    def step2(b):
        for i in range(3):
            arrived(r1x.at[b, i], r1x_r.at[b, i])
            arrived(r1y.at[b, i], r1y_r.at[b, i])
        from_a = (r1x[b, 0].astype(F32) + r1x[b, 1].astype(F32)) + r1x[b, 2].astype(F32)
        from_b = (r1y[b, 0].astype(F32) + r1y[b, 1].astype(F32)) + r1y[b, 2].astype(F32)
        s1x[b] = pb[b, :, ca, 0:32] + from_a.reshape(4, 32, BLK)
        s1y[b] = pb[b, cb, :, 32:56] + from_b.reshape(4, 24, BLK)
        for k in (2, 1, 3):
            z2x[b, k - 1] = s1x[b, lax.rem(cb + k, 4)].astype(BF16)
            tail = jnp.zeros((8, BLK), F32)
            z2y[b, k - 1] = jnp.concatenate([s1y[b, lax.rem(ca + k, 4)], tail], axis=0).astype(BF16)
            for cp in copies2(b, k):
                cp.start()

    def step3(b):
        for k in (1, 2, 3):
            arrived(r2x.at[b, k - 1], r2x_r.at[b, k - 1])
            arrived(r2y.at[b, k - 1], r2y_r.at[b, k - 1])
        from_b = (r2x[b, 0].astype(F32) + r2x[b, 1].astype(F32)) + r2x[b, 2].astype(F32)
        from_a = (r2y[b, 0].astype(F32) + r2y[b, 1].astype(F32)) + r2y[b, 2].astype(F32)
        s2[b, 0:32] = s1x[b, cb] + from_b
        s2[b, 32:56] = s1y[b, ca] + from_a[0:24]

        @pl.when(mine(b))
        def _():
            fin[b // NB, z, lax.rem(block_of(b), 2)] = s2[b]

        @pl.when(jnp.logical_not(mine(b)))
        def _():
            copy3(b).start()

    def group_term(g, i, half):
        term = jnp.dot(
            hid_t[128 * i : 128 * (i + 1), pl.ds(mult(g * TG, TG), TG)],
            gs[pl.ds(mult(g * TG, TG), TG), 1024 * half : 1024 * (half + 1)],
            preferred_element_type=F32,
        )
        return term.astype(BF16).astype(F32)

    def add_group(g, half):
        for i in range(7):
            rows = slice(128 * i, 128 * (i + 1))
            cols = slice(1024 * half, 1024 * (half + 1))
            new = acc[rows, cols] + group_term(g, i, half)
            acc[rows, cols] = new
            out = new.astype(BF16)
            for j in range(2):
                at = mult(COLS * order[2 * half + j], COLS)
                gh[rows, pl.ds(at, COLS)] = out[:, COLS * j : COLS * (j + 1)]

    def when(condition, step, *args):
        @pl.when(condition)
        def _():
            step(*args)

    alone_blocks()
    hand_on(0)

    def early2(i):
        step2(NB - NX + i)
        step2(NB + i)

    def early3(i):
        step3(NB - NX + i)
        step3(NB + i)

    def late_waits():
        g_wait(6, 2)
        g_wait(7, 2)

    def block(i, _):
        when(i < 5, step1, i)
        when(i < 4, hand_on, i + 1)
        when((i > 1) & (i < 5), early2, i - 2)
        when((i > 2) & (i < 8), step2, i - 3)
        when(i == 5, hand_on, 5)
        when(i == 6, g_wait, 5, 2)
        when(i == 8, step3, 3)
        when(i == 8, step3, 4)
        when(i == 8, hand_on, 7)
        when(i == 8, late_waits)
        g = (i - 1 - i // 5) // 2
        first = (i == 1) | (i == 3) | (i == 6) | (i == 8)
        when(first, add_group, g, 0)
        when((i > 0) & (i != 5) & jnp.logical_not(first), add_group, g, 1)
        when((i > 4) & (i < 8), early3, i - 5)
        when(i == 6, step3, 0)
        when(i == 7, step3, 1)
        when(i == 7, step3, 2)
        when(i == 7, hand_on, 6)
        return 0

    lax.fori_loop(0, 10, block, 0)

    for half in range(2):
        cols = slice(128 * half, 128 * (half + 1))
        for k in range(4):

            @pl.when(jnp.logical_not((t == z) & (z == k)))
            def _():
                arrived(fin.at[0, k, half], f_r.at[0, k, half])

        near = (fin[0, 0, half] + fin[0, 1, half]) + (fin[0, 2, half] + fin[0, 3, half])
        alone = 2 * t + half >= NB - NX

        @pl.when(jnp.logical_not(alone))
        def _():
            hg[:, cols] = near.astype(BF16)

        @pl.when(alone)
        def _():
            for k in range(4):

                @pl.when(jnp.logical_not((lax.rem(t + 2, 4) == z) & (z == k)))
                def _():
                    arrived(fin.at[1, k, half], f_r.at[1, k, half])

            rest = (fin[1, 0, half] + fin[1, 1, half]) + (fin[1, 2, half] + fin[1, 3, half])
            hg[:, cols] = (near + rest).astype(BF16)

    for cp in (h_cross, h_pair, h_sib, fwd1, fwd2, h_hx):
        cp.wait_send()

    def drain(k, _):
        spread_copy(k).wait_send()
        ta_copy(k).wait_send()
        tb_copy(k).wait_send()
        t1_copy(k).wait_send()
        t2_copy(k).wait_send()
        la_copy(k).wait_send()
        lb_copy(k).wait_send()
        lc_copy(k).wait_send()
        return 0

    lax.fori_loop(1, 16, drain, 0)

    def drain_blocks(b, _):
        g_cross(b).wait_send()
        g_sib(b).wait_send()
        g_fwd(b).wait_send()
        return 0

    def drain_sums(n, _):
        for k in (1, 2, 3):
            for cp in copies1(n, k) + copies2(n, k):
                cp.wait_send()

        @pl.when(jnp.logical_not(mine(n)))
        def _():
            copy3(n).wait_send()

        return 0

    lax.fori_loop(0, NS, drain_sums, 0)
    lax.fori_loop(0, NB, drain_blocks, 0)


def hand_over(hg_in, gh_in, hg, gh, sem):
    a = pltpu.make_async_copy(hg_in, hg, sem.at[0])
    b = pltpu.make_async_copy(gh_in, gh, sem.at[1])
    a.start()
    b.start()
    a.wait()
    b.wait()


def body(hidden_states, student_head, teacher_logits, quality):
    teach = (
        teacher_logits.reshape(4, 256, 4, 128).transpose(1, 2, 0, 3).reshape(4, 16, 4, 16, 128)
    )
    hbm = pl.BlockSpec(memory_space=pltpu.HBM)
    vmem = pl.BlockSpec(memory_space=pltpu.VMEM)
    dma = pltpu.SemaphoreType.DMA
    hg, gh = pl.pallas_call(
        kernel,
        name="distill_backward",
        out_shape=(pltpu.VMEM((ROWS, TG), BF16), pltpu.VMEM((DS, 2048), BF16)),
        in_specs=[hbm, hbm, hbm, vmem],
        out_specs=(vmem, vmem),
        scratch_shapes=[
            pltpu.VMEM((TOK, D), BF16),
            pltpu.VMEM((DS, 2048), BF16),
            pltpu.VMEM((4, DS, COLS), BF16),
            pltpu.VMEM((DS, 2 * COLS), BF16),
            pltpu.VMEM((4, 16, 4, 16, 128), BF16),
            pltpu.VMEM((8, 2, 4, 4, 16, 128), BF16),
            pltpu.VMEM((16, 8, 2, 16, 128), BF16),
            pltpu.VMEM((TOK, COLS), F32),
            pltpu.VMEM((TOK, 2048), BF16),
            pltpu.VMEM((DS, TOK), BF16),
            pltpu.VMEM((DS, 2048), F32),
            pltpu.VMEM((NS, 4, 4, ROWS, BLK), F32),
            pltpu.VMEM((NS, 3, 128, BLK), BF16),
            pltpu.VMEM((NS, 3, 96, BLK), BF16),
            pltpu.VMEM((NS, 3, 128, BLK), BF16),
            pltpu.VMEM((NS, 3, 96, BLK), BF16),
            pltpu.VMEM((NS, 4, 32, BLK), F32),
            pltpu.VMEM((NS, 4, 24, BLK), F32),
            pltpu.VMEM((NS, 3, 32, BLK), BF16),
            pltpu.VMEM((NS, 3, 32, BLK), BF16),
            pltpu.VMEM((NS, 3, 32, BLK), BF16),
            pltpu.VMEM((NS, 3, 32, BLK), BF16),
            pltpu.VMEM((NS, ROWS, BLK), F32),
            pltpu.VMEM((2, 4, 2, ROWS, BLK), F32),
            pltpu.VMEM((1, 128), F32),
            pltpu.VMEM((15, 1, 128), F32),
            pltpu.VMEM((16, 1, 128), F32),
            pltpu.VMEM((16, 1, 128), F32),
            pltpu.VMEM((15, 1, 128), F32),
            pltpu.VMEM((1, 128), F32),
            pltpu.VMEM((15, 1, 128), F32),
            pltpu.VMEM((16, 1, 128), F32),
            pltpu.VMEM((16, 1, 128), F32),
            dma((10,)),
            dma((4, 3)), dma((4, 4)),
            dma((1,)), dma((1,)),
            dma((5,)), dma((5,)),
            dma((15,)), dma((15,)),
            dma((15,)), dma((15,)),
            dma((16,)), dma((16,)),
            dma((15,)), dma((15,)),
            dma((15,)), dma((15,)),
            dma((15,)), dma((15,)),
            dma((15,)), dma((15,)),
            dma((15,)), dma((15,)),
            dma((NB, 3)), dma((NB, 3)),
            dma((NS, 3)), dma((NS, 3)),
            dma((NS, 3)), dma((NS, 3)),
            dma((NS, 3)), dma((NS, 3)),
            dma((NS, 3)), dma((NS, 3)),
            dma((NS,)), dma((2, 4, 2)),
        ],
        compiler_params=pltpu.CompilerParams(
            collective_id=0, has_side_effects=True, vmem_limit_bytes=55 * 2**20
        ),
        cost_estimate=pl.CostEstimate(
            flops=3 * 2 * TOK * DS * 2048, bytes_accessed=15 * 2**20, transcendentals=2**21
        ),
    )(hidden_states, student_head, teach, quality.reshape(2, 128))
    hg, gh = pl.pallas_call(
        hand_over,
        name="results",
        out_shape=(
            jax.ShapeDtypeStruct((ROWS, TG), BF16),
            jax.ShapeDtypeStruct((DS, 2048), BF16),
        ),
        in_specs=[vmem, vmem],
        out_specs=(hbm, hbm),
        scratch_shapes=[dma((2,))],
        compiler_params=pltpu.CompilerParams(vmem_limit_bytes=2**20),
    )(
        pltpu.with_memory_space_constraint(hg, pltpu.VMEM),
        pltpu.with_memory_space_constraint(gh, pltpu.VMEM),
    )
    return hg.T, gh


def solution(mesh):
    return jax.shard_map(
        body,
        mesh=mesh,
        in_specs=(P("tok", None), P("tok", "voc"), P(("tok", "voc"), None), P("tok")),
        out_specs=(P("tok", "voc"), P("tok", "voc")),
        check_vma=False,
    )
```

```python
import functools

import jax
import jax.numpy as jnp
from jax import lax
from jax.experimental import pallas as pl
from jax.experimental.pallas import tpu as pltpu
from jax.sharding import PartitionSpec as P

MESH = pl.DeviceIdType.MESH
LOSS_SCALE = 64.0
D = 3584
DS = 896
TOK = 1024
TG = 256
COLS = 512
BLK = 128
TB_SPLIT = 8
NB = 8
NX = 3
NS = NB + NX
ROWS = 56
CHUNKS = ((0, 256), (256, 256), (512, 256), (768, 128))
F32 = jnp.float32
BF16 = jnp.bfloat16


def mult(x, m):
    return pl.multiple_of(x, m)


def kernel(
    hid, head, teach, qual_hbm, hg, gh,
    hid_all, headv, hcols, hxc, tloc, ta, tb, stu, gs, hid_t, acc,
    pb, zx, zy, r1x, r1y, s1x, s1y, z2x, z2y, r2x, r2y, s2, fin,
    qual, row_a, got_t, tq, st, got_a, row_b, got_b, full, scale,
    loc, head_s, head_r, hx_s, hx_r, hid_s, hid_r, bc_s, bc_r, ta_s, ta_r, tb_s, tb_r,
    t1_s, t1_r, t2_s, t2_r, la_s, la_r, lb_s, lb_r, lc_s, lc_r, g_s, g_r,
    r1x_s, r1x_r, r1y_s, r1y_r, r2x_s, r2x_r, r2y_s, r2y_r, f_s, f_r,
):
    t = lax.axis_index("tok")
    v = lax.axis_index("voc")
    z = v // 16
    p = v % 16
    y = p // 4
    x = p % 4
    c = t // 2
    h = t % 2
    sib = c * 2 + (1 - h)
    cross = (1 - c) * 2 + h
    diag = (1 - c) * 2 + (1 - h)
    tz = t * 4 + z

    def plane_peer(k):
        return (t, z * 16 + lax.rem(p + k, 16))

    def tz_peer(k):
        q = lax.rem(tz + k, 16)
        return (q // 4, (q % 4) * 16 + p)

    def remote(src, dst, ss, rs, dev):
        return pltpu.make_async_remote_copy(
            src_ref=src, dst_ref=dst, send_sem=ss, recv_sem=rs, device_id=dev, device_id_type=MESH
        )

    def arrived(ref, sem):
        pltpu.make_async_copy(ref, ref, sem).wait()

    bar = pltpu.get_barrier_semaphore()

    def greet(k, _):
        pl.semaphore_signal(bar, inc=1, device_id=plane_peer(k), device_id_type=MESH)
        pl.semaphore_signal(bar, inc=1, device_id=tz_peer(k), device_id_type=MESH)
        return 0

    lax.fori_loop(1, 16, greet, 0)

    c_own = pltpu.make_async_copy(head.at[:, pl.ds(mult(COLS * t, COLS), COLS)], hcols.at[t], loc.at[0])
    c_hid = pltpu.make_async_copy(hid, hid_all.at[pl.ds(mult(TG * t, TG), TG)], loc.at[1])
    order = (t, sib, cross, diag)
    c_heads = [
        pltpu.make_async_copy(
            head.at[:, pl.ds(mult(COLS * dev, COLS), COLS)], headv.at[:, pl.ds(COLS * j, COLS)], loc.at[5 + j]
        )
        for j, dev in enumerate(order)
    ]
    c_tl = pltpu.make_async_copy(teach, tloc, loc.at[3])
    c_ta = pltpu.make_async_copy(teach.at[:, p], ta.at[p // 2, p % 2], loc.at[4])
    c_q = pltpu.make_async_copy(qual_hbm, qual, loc.at[10])
    for cp in (c_hid, c_own, c_tl, c_ta, c_q, *c_heads):
        cp.start()

    pl.semaphore_wait(bar, 30)

    def piece(group, q):
        return (
            pl.ds(mult(TG * group + 16 * (q // 2), 16), 16),
            pl.ds(mult(1792 * (q % 2), 128), 1792),
        )

    pr, pc = piece(0, p)
    mr, mc = piece(t, p)
    znb = lax.rem(z + 2 * c + 3, 4)
    h_cross = remote(
        hid.at[pr, pc], hid_all.at[mr, mc], hid_s.at[0], hid_r.at[0], (cross, znb * 16 + p)
    )
    h_cross.start()
    h_pair = remote(
        hid.at[pl.ds(128, 128)], hid_all.at[pl.ds(mult(TG * t + 128, 128), 128)],
        hid_s.at[1], hid_r.at[1], (cross, znb * 16 + p),
    )
    h_sib = remote(
        hid, hid_all.at[pl.ds(mult(TG * t, TG), TG)], hid_s.at[2], hid_r.at[2], (sib, v)
    )
    heads = []
    for i, (r0, rn) in enumerate(CHUNKS):
        for j, dev in enumerate((cross, diag, sib)):
            heads.append(
                remote(
                    head.at[pl.ds(r0, rn), pl.ds(mult(COLS * dev, COLS), COLS)],
                    hcols.at[t, pl.ds(r0, rn)],
                    head_s.at[i, j], head_r.at[t, i], (dev, v),
                )
            )
    for cp in heads[:3]:
        cp.start()
    h_pair.start()
    h_sib.start()
    for cp in heads[3:]:
        cp.start()

    xr, xc = piece(cross, p)
    arrived(hid_all.at[xr, xc], hid_r.at[0])

    def spread_copy(k):
        return remote(
            hid_all.at[xr, xc], hid_all.at[xr, xc], bc_s.at[k - 1], bc_r.at[k - 1], plane_peer(k)
        )

    def ta_copy(k):
        q = lax.rem(p + k, 16)
        return remote(
            teach.at[:, q], ta.at[p // 2, p % 2], ta_s.at[k - 1], ta_r.at[k - 1], plane_peer(k)
        )

    def start_spread(k, _):
        spread_copy(k).start()
        return 0

    def start_ta(k, _):
        ta_copy(k).start()
        return 0

    lax.fori_loop(1, 16, start_spread, 0)
    lax.fori_loop(1, 16, start_ta, 0)

    c_tl.wait()

    def tl_tile(i):
        return tloc[i // 4, pl.ds(mult((i % 4) * 4, 4), 4)].astype(F32)

    def top_step(i, m):
        return jnp.maximum(m, jnp.max(tl_tile(i), axis=(0, 1)))

    top16 = lax.fori_loop(0, 16, top_step, jnp.full((16, 128), -jnp.inf, F32))
    top16 = jnp.max(top16, axis=1, keepdims=True)
    top4 = jnp.maximum(jnp.maximum(top16[0:4], top16[4:8]), jnp.maximum(top16[8:12], top16[12:16]))
    top16 = jnp.concatenate([top4] * 4, axis=0)
    top_full = jnp.broadcast_to(top16, (16, 128))

    def sum_step(i, s):
        return s + jnp.sum(jnp.exp(tl_tile(i) - top_full), axis=(0, 1))

    sum16 = lax.fori_loop(0, 16, sum_step, jnp.zeros((16, 128), F32))
    sum16 = jnp.sum(sum16, axis=1, keepdims=True)
    sum4 = sum16[0:4] + sum16[4:8] + sum16[8:12] + sum16[12:16]
    lse4 = top4 + jnp.log(sum4)
    lane = lax.broadcasted_iota(jnp.int32, (1, 128), 1)
    low = lane < 64
    trow = jnp.zeros((1, 128), F32)
    for r in range(4):
        trow = jnp.where(lane == 4 * p + r, jnp.broadcast_to(lse4[r : r + 1], (1, 128)), trow)
    row_a[...] = trow

    def swap(a):
        return pltpu.roll(a, 64, len(a.shape) - 1)

    def t1_copy(k):
        return remote(row_a, got_t.at[k - 1], t1_s.at[k - 1], t1_r.at[k - 1], plane_peer(k))

    def t2_copy(k):
        return remote(tq.at[tz], tq.at[tz], t2_s.at[k - 1], t2_r.at[k - 1], tz_peer(k))

    def start_t1(k, _):
        t1_copy(k).start()
        return 0

    def start_t2(k, _):
        t2_copy(k).start()
        return 0

    lax.fori_loop(1, 16, start_t1, 0)

    def clear(i, _):
        acc[pl.ds(mult(i * 64, 64), 64), :] = jnp.zeros((64, 2048), F32)
        return 0

    lax.fori_loop(0, 14, clear, 0)

    def wait_t1(k, _):
        arrived(got_t.at[k - 1], t1_r.at[k - 1])
        return 0

    lax.fori_loop(1, 16, wait_t1, 0)
    tl_row = row_a[...] + jnp.sum(got_t[...], axis=0)
    c_q.wait()
    q_row = qual[pl.ds(z // 2, 1), :]
    weight = LOSS_SCALE * jnp.where(lax.rem(z, 2) == 0, q_row, swap(q_row))
    tq[tz] = jnp.where(low, tl_row - jnp.log(weight), swap(weight))
    lax.fori_loop(1, 16, start_t2, 0)

    gx = mult(TG * cross, TG)

    def wait_spread(k, _):
        ar, ac = piece(cross, lax.rem(p + 16 - k, 16))
        arrived(hid_all.at[ar, ac], bc_r.at[k - 1])
        return 0

    lax.fori_loop(1, 16, wait_spread, 0)
    fwd1 = remote(
        hid_all.at[pl.ds(gx, 128)], hid_all.at[pl.ds(gx, 128)], hid_s.at[3], hid_r.at[3], (sib, v)
    )
    fwd1.start()
    gx2 = mult(TG * cross + 128, 128)
    arrived(hid_all.at[pl.ds(gx2, 128)], hid_r.at[1])
    fwd2 = remote(
        hid_all.at[pl.ds(gx2, 128)], hid_all.at[pl.ds(gx2, 128)], hid_s.at[4], hid_r.at[4], (sib, v)
    )
    fwd2.start()
    c_hid.wait()
    arrived(hid_all.at[pl.ds(mult(TG * sib, TG), TG)], hid_r.at[2])
    arrived(hid_all.at[pl.ds(mult(TG * diag, 128), 128)], hid_r.at[3])
    arrived(hid_all.at[pl.ds(mult(TG * diag + 128, 128), 128)], hid_r.at[4])

    def multiply(slot, r0, rn, first):
        base = mult(DS * slot + r0, 128)

        term = jnp.dot(
            hid_all[:, pl.ds(base, rn)], hcols[slot, pl.ds(r0, rn), :], preferred_element_type=F32
        )
        if first:
            stu[...] = term
        else:
            stu[...] += term

    def wait_head(slot, i):
        r0, rn = CHUNKS[i]
        arrived(hcols.at[slot, pl.ds(r0, rn)], head_r.at[slot, i])

    c_own.wait()
    multiply(t, 0, DS, True)
    for i in range(4):
        wait_head(sib, i)
    multiply(sib, 0, DS, False)

    def turn(i, _):
        rows = pl.ds(mult(i * 128, 128), 128)
        for j in range(7):
            block = hid_all[rows, pl.ds(mult(DS * t + 128 * j, 128), 128)]
            hid_t[128 * j : 128 * (j + 1), rows] = block.astype(F32).T.astype(BF16)
        return 0

    lax.fori_loop(0, 8, turn, 0)

    for i in range(3):
        r0, rn = CHUNKS[i]
        wait_head(cross, i)
        multiply(cross, r0, rn, False)
        wait_head(diag, i)
        multiply(diag, r0, rn, False)

    c_ta.wait()

    def wait_ta(k, _):
        q = lax.rem(p + 16 - k, 16)
        arrived(ta.at[q // 2, q % 2], ta_r.at[k - 1])
        return 0

    lax.fori_loop(1, 16, wait_ta, 0)
    def tb_copy(k):
        q = lax.rem(tz + k, 16)
        return remote(
            ta.at[:, :, q % 4, q // 4], tb.at[tz], tb_s.at[k], tb_r.at[tz], tz_peer(k)
        )

    def is_early(k):
        q = lax.rem(tz + k, 16)
        t2, zq = q // 4, q % 4
        return ((t2 // 2 != c) & (zq == znb)) | ((t2 == sib) & (zq == z))

    def start_tb(k, _):
        @pl.when(jnp.logical_not(is_early(k)))
        def _():
            tb_copy(k).start()

        return 0

    def start_early(k, _):
        @pl.when(is_early(k))
        def _():
            tb_copy(k).start()

        return 0

    lax.fori_loop(1, 16, start_early, 0)
    wait_head(cross, 3)
    wait_head(diag, 3)
    for cp in heads:
        cp.wait_send()
    lax.fori_loop(1, TB_SPLIT, start_tb, 0)
    c_tb = pltpu.make_async_copy(ta.at[:, :, z, t], tb.at[tz], tb_r.at[tz])
    c_tb.start()

    c_hx = pltpu.make_async_copy(hcols.at[cross], hxc.at[:, pl.ds(0, COLS)], loc.at[9])
    c_hx.start()
    h_hx = remote(hcols.at[diag], hxc.at[:, pl.ds(COLS, COLS)], hx_s.at[0], hx_r.at[0], (sib, v))
    h_hx.start()

    r0, rn = CHUNKS[3]
    multiply(cross, r0, rn, False)
    multiply(diag, r0, rn, False)

    def stats(b, _):
        rows = pl.ds(mult(b * BLK, BLK), BLK)
        val = stu[rows, :]
        top = jnp.max(val, axis=1, keepdims=True)
        e = jnp.exp(val - top)
        stu[rows, :] = e
        tot = jnp.sum(e, axis=1, keepdims=True)
        both = jnp.where(jnp.broadcast_to(low, (BLK, BLK)), top, tot).T
        m_row, s_row = both[0:1, :], both[64:65, :]
        st[2 * b] = jnp.where(low, m_row, swap(s_row))
        st[2 * b + 1] = jnp.where(low, swap(m_row), s_row)
        return 0

    lax.fori_loop(0, NB, stats, 0, unroll=4)

    def la_copy(k):
        return remote(
            st.at[lax.rem(p + k, 16)], got_a.at[k - 1], la_s.at[k - 1], la_r.at[k - 1], plane_peer(k)
        )

    def lb_copy(k):
        return remote(row_b, got_b.at[k - 1], lb_s.at[k - 1], lb_r.at[k - 1], tz_peer(k))

    def lc_copy(k):
        return remote(full.at[p], full.at[p], lc_s.at[k - 1], lc_r.at[k - 1], plane_peer(k))

    def start_la(k, _):
        la_copy(k).start()
        return 0

    def start_lb(k, _):
        lb_copy(k).start()
        return 0

    def start_lc(k, _):
        lc_copy(k).start()
        return 0

    def combine(mine, got):
        top = jnp.maximum(mine, jnp.max(got, axis=0))
        tot = swap(mine) * jnp.exp(mine - top) + jnp.sum(swap(got) * jnp.exp(got - top[None]), axis=0)
        return jnp.where(low, top, swap(tot))

    lax.fori_loop(1, 16, start_la, 0)

    def wait_la(k, _):
        arrived(got_a.at[k - 1], la_r.at[k - 1])
        return 0

    lax.fori_loop(1, 16, wait_la, 0)
    row_b[...] = combine(st[p], got_a[...])
    lax.fori_loop(1, 16, start_lb, 0)
    lax.fori_loop(TB_SPLIT, 16, start_tb, 0)

    def wait_lb(k, _):
        arrived(got_b.at[k - 1], lb_r.at[k - 1])
        return 0

    lax.fori_loop(1, 16, wait_lb, 0)
    full[p] = combine(row_b[...], got_b[...])
    lax.fori_loop(1, 16, start_lc, 0)

    def wait_t2(k, _):
        q = lax.rem(tz + 16 - k, 16)
        arrived(tq.at[q], t2_r.at[k - 1])
        return 0

    def wait_lc(k, _):
        q = lax.rem(p + 16 - k, 16)
        arrived(full.at[q], lc_r.at[k - 1])
        return 0

    lax.fori_loop(1, 16, wait_t2, 0)
    lax.fori_loop(1, 16, wait_lc, 0)
    scale[...] = swap(tq[...]) * jnp.exp(st[...] - full[...]) / swap(full[...])

    def g_copy(b, j, src, dst, dev):
        rows = pl.ds(mult(b * BLK, BLK), BLK)
        return remote(
            gs.at[rows, pl.ds(COLS * src, COLS)], gs.at[rows, pl.ds(COLS * dst, COLS)],
            g_s.at[b, j], g_r.at[b, j], (dev, v),
        )

    def g_cross(b):
        return g_copy(b, 0, 0, 2, cross)

    def g_sib(b):
        return g_copy(b, 1, 0, 1, sib)

    def g_fwd(b):
        return g_copy(b, 2, 2, 3, sib)

    def g_wait(b, j):
        slot = (2, 1, 3)[j]
        rows = pl.ds(mult(b * BLK, BLK), BLK)
        arrived(gs.at[rows, pl.ds(COLS * slot, COLS)], g_r.at[b, j])

    sub = lax.broadcasted_iota(jnp.int32, (16, 8, 128), 1) < 4

    def make_grads(b, _):
        rows = pl.ds(mult(b * BLK, BLK), BLK)
        for s in range(2):
            arrived(tb.at[2 * b + s], tb_r.at[2 * b + s])
        even = tb[pl.ds(mult(2 * b, 2), 2), :, 0].astype(F32).reshape(16, 16, 128)
        odd = tb[pl.ds(mult(2 * b, 2), 2), :, 1].astype(F32).reshape(16, 16, 128)
        sc_row = jnp.where(low, scale[2 * b], swap(scale[2 * b + 1]))
        tl_row = jnp.where(low, tq[2 * b], swap(tq[2 * b + 1]))
        sc = jnp.broadcast_to(sc_row, (BLK, BLK)).T
        tl = jnp.broadcast_to(tl_row, (BLK, BLK)).T
        for q in range(4):
            half = slice(8 * (q // 2), 8 * (q // 2) + 8)
            lo, hi = even[:, half], odd[:, half]
            if q % 2 == 0:
                mixed = jnp.where(sub, lo, pltpu.roll(hi, 4, 1))
            else:
                mixed = jnp.where(sub, pltpu.roll(lo, 4, 1), hi)
            teacher = mixed.reshape(BLK, 128)
            e = stu[rows, 128 * q : 128 * (q + 1)]
            g = e * sc - jnp.exp(teacher - tl)
            gs[rows, 128 * q : 128 * (q + 1)] = g.astype(BF16)
        g_sib(b).start()

        @pl.when(b < NB - NX)
        def _():
            g_cross(b).start()

        return 0

    lax.fori_loop(0, NB, make_grads, 0)
    for b in range(NB - NX, NB):
        g_cross(b).start()
    c_hx.wait()
    arrived(hxc.at[:, pl.ds(COLS, COLS)], hx_r.at[0])
    for cp in c_heads:
        cp.wait()

    ca = x + h * (y - x)
    cb = y + h * (x - y)

    def line_a(k):
        return (t, z * 16 + (1 - h) * (y * 4 + lax.rem(x + k, 4)) + h * (lax.rem(y + k, 4) * 4 + x))

    def line_b(k):
        return (t, z * 16 + h * (y * 4 + lax.rem(x + k, 4)) + (1 - h) * (lax.rem(y + k, 4) * 4 + x))

    def copies1(b, k):
        i = k - 1
        return (
            remote(zx.at[b, i], r1x.at[b, i], r1x_s.at[b, i], r1x_r.at[b, i], line_a(k)),
            remote(zy.at[b, i], r1y.at[b, i], r1y_s.at[b, i], r1y_r.at[b, i], line_b(k)),
        )

    def copies2(b, k):
        i = k - 1
        return (
            remote(z2x.at[b, i], r2x.at[b, i], r2x_s.at[b, i], r2x_r.at[b, i], line_b(k)),
            remote(z2y.at[b, i], r2y.at[b, i], r2y_s.at[b, i], r2y_r.at[b, i], line_a(k)),
        )

    def block_of(n):
        return n - NX * (n // NB)

    def run_of(n):
        return t + (n // NB) * (cross - t)

    def copy3(n):
        b = block_of(n)
        at = (n // NB, z, lax.rem(b, 2))
        return remote(s2.at[n], fin.at[at], f_s.at[n], f_r.at[at], (b // 2, run_of(n) * 16 + p))

    def mine(n):
        return (block_of(n) // 2 == t) & (run_of(n) == z)

    def hand_on(b):
        g_wait(b, 0)
        g_fwd(b).start()

    def dot_t(a, b):
        return lax.dot_general(a, b, (((1,), (1,)), ((), ())), preferred_element_type=F32)

    def step1(b):
        rows = pl.ds(mult(b * BLK, BLK), BLK)
        g_wait(b, 1)
        g_wait(b, 2)
        keep(b, dot_t(headv[...], gs[rows, :]), 0)
        spread(b)

    def alone_blocks():
        for b in range(NB - NX, NB):
            g_wait(b, 1)
        for n, rows_of in ((NB - NX, headv), (NB, hxc)):
            for m in range(2):
                out = dot_t(
                    rows_of[448 * m : 448 * (m + 1), 0 : 2 * COLS],
                    gs[BLK * (NB - NX) :, 0 : 2 * COLS],
                )
                for k in range(NX):
                    keep(n + k, out[:, BLK * k : BLK * (k + 1)], 2 * m)
        for k in range(NX):
            spread(NB - NX + k)
            spread(NB + k)

    def keep(n, out, begin):
        for i in range(begin, begin + out.shape[0] // (4 * ROWS)):
            for j in range(4):
                first = ROWS * (4 * (i - begin) + j)
                pb[n, i + h * (j - i), j + h * (i - j)] = out[first : first + ROWS]

    def spread(b):
        for k in (2, 1, 3):
            to_a, to_b = lax.rem(ca + k, 4), lax.rem(cb + k, 4)
            zx[b, k - 1] = pb[b, :, to_a, 0:32].reshape(128, BLK).astype(BF16)
            zy[b, k - 1] = pb[b, to_b, :, 32:56].reshape(96, BLK).astype(BF16)
            for cp in copies1(b, k):
                cp.start()

    def step2(b):
        for i in range(3):
            arrived(r1x.at[b, i], r1x_r.at[b, i])
            arrived(r1y.at[b, i], r1y_r.at[b, i])
        from_a = (r1x[b, 0].astype(F32) + r1x[b, 1].astype(F32)) + r1x[b, 2].astype(F32)
        from_b = (r1y[b, 0].astype(F32) + r1y[b, 1].astype(F32)) + r1y[b, 2].astype(F32)
        s1x[b] = pb[b, :, ca, 0:32] + from_a.reshape(4, 32, BLK)
        s1y[b] = pb[b, cb, :, 32:56] + from_b.reshape(4, 24, BLK)
        for k in (2, 1, 3):
            z2x[b, k - 1] = s1x[b, lax.rem(cb + k, 4)].astype(BF16)
            tail = jnp.zeros((8, BLK), F32)
            z2y[b, k - 1] = jnp.concatenate([s1y[b, lax.rem(ca + k, 4)], tail], axis=0).astype(BF16)
            for cp in copies2(b, k):
                cp.start()

    def step3(b):
        for k in (1, 2, 3):
            arrived(r2x.at[b, k - 1], r2x_r.at[b, k - 1])
            arrived(r2y.at[b, k - 1], r2y_r.at[b, k - 1])
        from_b = (r2x[b, 0].astype(F32) + r2x[b, 1].astype(F32)) + r2x[b, 2].astype(F32)
        from_a = (r2y[b, 0].astype(F32) + r2y[b, 1].astype(F32)) + r2y[b, 2].astype(F32)
        s2[b, 0:32] = s1x[b, cb] + from_b
        s2[b, 32:56] = s1y[b, ca] + from_a[0:24]

        @pl.when(mine(b))
        def _():
            fin[b // NB, z, lax.rem(block_of(b), 2)] = s2[b]

        @pl.when(jnp.logical_not(mine(b)))
        def _():
            copy3(b).start()

    def group_term(g, i, half):
        term = jnp.dot(
            hid_t[128 * i : 128 * (i + 1), pl.ds(mult(g * TG, TG), TG)],
            gs[pl.ds(mult(g * TG, TG), TG), 1024 * half : 1024 * (half + 1)],
            preferred_element_type=F32,
        )
        return term.astype(BF16).astype(F32)

    def add_group(g, half):
        for i in range(7):
            rows = slice(128 * i, 128 * (i + 1))
            cols = slice(1024 * half, 1024 * (half + 1))
            new = acc[rows, cols] + group_term(g, i, half)
            acc[rows, cols] = new
            out = new.astype(BF16)
            for j in range(2):
                at = mult(COLS * order[2 * half + j], COLS)
                gh[rows, pl.ds(at, COLS)] = out[:, COLS * j : COLS * (j + 1)]

    def when(condition, step, *args):
        @pl.when(condition)
        def _():
            step(*args)

    alone_blocks()
    hand_on(0)

    def early2(i):
        step2(NB - NX + i)
        step2(NB + i)

    def early3(i):
        step3(NB - NX + i)
        step3(NB + i)

    def late_waits():
        g_wait(6, 2)
        g_wait(7, 2)

    def block(i, _):
        when(i < 5, step1, i)
        when(i < 4, hand_on, i + 1)
        when((i > 1) & (i < 5), early2, i - 2)
        when((i > 2) & (i < 8), step2, i - 3)
        when(i == 5, hand_on, 5)
        when(i == 6, g_wait, 5, 2)
        when(i == 8, step3, 3)
        when(i == 8, step3, 4)
        when(i == 8, hand_on, 7)
        when(i == 8, late_waits)
        g = (i - 1 - i // 5) // 2
        first = (i == 1) | (i == 3) | (i == 6) | (i == 8)
        when(first, add_group, g, 0)
        when((i > 0) & (i != 5) & jnp.logical_not(first), add_group, g, 1)
        when((i > 4) & (i < 8), early3, i - 5)
        when(i == 6, step3, 0)
        when(i == 7, step3, 1)
        when(i == 7, step3, 2)
        when(i == 7, hand_on, 6)
        return 0

    lax.fori_loop(0, 10, block, 0)

    for cp in (h_cross, h_pair, h_sib, fwd1, fwd2, h_hx):
        cp.wait_send()

    def drain(k, _):
        spread_copy(k).wait_send()
        ta_copy(k).wait_send()
        tb_copy(k).wait_send()
        t1_copy(k).wait_send()
        t2_copy(k).wait_send()
        la_copy(k).wait_send()
        lb_copy(k).wait_send()
        lc_copy(k).wait_send()
        return 0

    lax.fori_loop(1, 16, drain, 0)

    def drain_blocks(b, _):
        g_cross(b).wait_send()
        g_sib(b).wait_send()
        g_fwd(b).wait_send()
        return 0

    def drain_sums(n, _):
        for k in (1, 2, 3):
            for cp in copies1(n, k) + copies2(n, k):
                cp.wait_send()

        @pl.when(jnp.logical_not(mine(n)))
        def _():
            copy3(n).wait_send()

        return 0

    lax.fori_loop(0, NS, drain_sums, 0)
    lax.fori_loop(0, NB, drain_blocks, 0)

    for half in range(2):
        cols = slice(128 * half, 128 * (half + 1))
        for k in range(4):

            @pl.when(jnp.logical_not((t == z) & (z == k)))
            def _():
                arrived(fin.at[0, k, half], f_r.at[0, k, half])

        near = (fin[0, 0, half] + fin[0, 1, half]) + (fin[0, 2, half] + fin[0, 3, half])
        alone = 2 * t + half >= NB - NX

        @pl.when(jnp.logical_not(alone))
        def _():
            hg[:, cols] = near.astype(BF16)

        @pl.when(alone)
        def _():
            for k in range(4):

                @pl.when(jnp.logical_not((lax.rem(t + 2, 4) == z) & (z == k)))
                def _():
                    arrived(fin.at[1, k, half], f_r.at[1, k, half])

            rest = (fin[1, 0, half] + fin[1, 1, half]) + (fin[1, 2, half] + fin[1, 3, half])
            hg[:, cols] = (near + rest).astype(BF16)


def hand_over(hg_in, gh_in, hg, gh, sem):
    copies = [pltpu.make_async_copy(hg_in, hg, sem.at[7])]
    for i in range(7):
        rows = pl.ds(128 * i, 128)
        copies.append(pltpu.make_async_copy(gh_in.at[rows], gh.at[rows], sem.at[i]))
    for cp in copies:
        cp.start()
    for cp in copies:
        cp.wait()


def body(hidden_states, student_head, teacher_logits, quality):
    teach = (
        teacher_logits.reshape(4, 256, 4, 128).transpose(1, 2, 0, 3).reshape(4, 16, 4, 16, 128)
    )
    hbm = pl.BlockSpec(memory_space=pltpu.HBM)
    vmem = pl.BlockSpec(memory_space=pltpu.VMEM)
    dma = pltpu.SemaphoreType.DMA
    hg, gh = pl.pallas_call(
        kernel,
        name="distill_backward",
        out_shape=(pltpu.VMEM((ROWS, TG), BF16), pltpu.VMEM((DS, 2048), BF16)),
        in_specs=[hbm, hbm, hbm, hbm],
        out_specs=(vmem, vmem),
        scratch_shapes=[
            pltpu.VMEM((TOK, D), BF16),
            pltpu.VMEM((DS, 2048), BF16),
            pltpu.VMEM((4, DS, COLS), BF16),
            pltpu.VMEM((DS, 2 * COLS), BF16),
            pltpu.VMEM((4, 16, 4, 16, 128), BF16),
            pltpu.VMEM((8, 2, 4, 4, 16, 128), BF16),
            pltpu.VMEM((16, 8, 2, 16, 128), BF16),
            pltpu.VMEM((TOK, COLS), F32),
            pltpu.VMEM((TOK, 2048), BF16),
            pltpu.VMEM((DS, TOK), BF16),
            pltpu.VMEM((DS, 2048), F32),
            pltpu.VMEM((NS, 4, 4, ROWS, BLK), F32),
            pltpu.VMEM((NS, 3, 128, BLK), BF16),
            pltpu.VMEM((NS, 3, 96, BLK), BF16),
            pltpu.VMEM((NS, 3, 128, BLK), BF16),
            pltpu.VMEM((NS, 3, 96, BLK), BF16),
            pltpu.VMEM((NS, 4, 32, BLK), F32),
            pltpu.VMEM((NS, 4, 24, BLK), F32),
            pltpu.VMEM((NS, 3, 32, BLK), BF16),
            pltpu.VMEM((NS, 3, 32, BLK), BF16),
            pltpu.VMEM((NS, 3, 32, BLK), BF16),
            pltpu.VMEM((NS, 3, 32, BLK), BF16),
            pltpu.VMEM((NS, ROWS, BLK), F32),
            pltpu.VMEM((2, 4, 2, ROWS, BLK), F32),
            pltpu.VMEM((2, 128), F32),
            pltpu.VMEM((1, 128), F32),
            pltpu.VMEM((15, 1, 128), F32),
            pltpu.VMEM((16, 1, 128), F32),
            pltpu.VMEM((16, 1, 128), F32),
            pltpu.VMEM((15, 1, 128), F32),
            pltpu.VMEM((1, 128), F32),
            pltpu.VMEM((15, 1, 128), F32),
            pltpu.VMEM((16, 1, 128), F32),
            pltpu.VMEM((16, 1, 128), F32),
            dma((11,)),
            dma((4, 3)), dma((4, 4)),
            dma((1,)), dma((1,)),
            dma((5,)), dma((5,)),
            dma((15,)), dma((15,)),
            dma((15,)), dma((15,)),
            dma((16,)), dma((16,)),
            dma((15,)), dma((15,)),
            dma((15,)), dma((15,)),
            dma((15,)), dma((15,)),
            dma((15,)), dma((15,)),
            dma((15,)), dma((15,)),
            dma((NB, 3)), dma((NB, 3)),
            dma((NS, 3)), dma((NS, 3)),
            dma((NS, 3)), dma((NS, 3)),
            dma((NS, 3)), dma((NS, 3)),
            dma((NS, 3)), dma((NS, 3)),
            dma((NS,)), dma((2, 4, 2)),
        ],
        compiler_params=pltpu.CompilerParams(
            collective_id=0, has_side_effects=True, vmem_limit_bytes=55 * 2**20
        ),
        cost_estimate=pl.CostEstimate(
            flops=3 * 2 * TOK * DS * 2048, bytes_accessed=15 * 2**20, transcendentals=2**21
        ),
    )(hidden_states, student_head, teach, quality.reshape(2, 128))
    hg, gh = pl.pallas_call(
        hand_over,
        name="results",
        out_shape=(
            jax.ShapeDtypeStruct((ROWS, TG), BF16),
            jax.ShapeDtypeStruct((DS, 2048), BF16),
        ),
        in_specs=[vmem, vmem],
        out_specs=(hbm, hbm),
        scratch_shapes=[dma((8,))],
        compiler_params=pltpu.CompilerParams(vmem_limit_bytes=2**20),
    )(
        pltpu.with_memory_space_constraint(hg, pltpu.VMEM),
        pltpu.with_memory_space_constraint(gh, pltpu.VMEM),
    )
    return hg.T, gh


def solution(mesh):
    return jax.shard_map(
        body,
        mesh=mesh,
        in_specs=(P("tok", None), P("tok", "voc"), P(("tok", "voc"), None), P("tok")),
        out_specs=(P("tok", "voc"), P("tok", "voc")),
        check_vma=False,
    )
```

```python
import functools

import jax
import jax.numpy as jnp
from jax import lax
from jax.experimental import pallas as pl
from jax.experimental.pallas import tpu as pltpu
from jax.sharding import PartitionSpec as P

MESH = pl.DeviceIdType.MESH
LOSS_SCALE = 64.0
D = 3584
DS = 896
TOK = 1024
TG = 256
COLS = 512
BLK = 128
TB_SPLIT = 8
NB = 8
NX = 3
NS = NB + NX
ROWS = 56
CHUNKS = ((0, 256), (256, 256), (512, 256), (768, 128))
F32 = jnp.float32
BF16 = jnp.bfloat16


def mult(x, m):
    return pl.multiple_of(x, m)


def kernel(
    hid, head, teach, qual_hbm, hg, gh,
    hid_all, headv, hcols, hxc, tloc, ta, tb, stu, gs, hid_t, acc,
    pb, zx, zy, r1x, r1y, s1x, s1y, z2x, z2y, r2x, r2y, s2, fin,
    qual, row_a, got_t, tq, st, got_a, row_b, got_b, full, scale,
    loc, head_s, head_r, hx_s, hx_r, hid_s, hid_r, bc_s, bc_r, ta_s, ta_r, tb_s, tb_r,
    t1_s, t1_r, t2_s, t2_r, la_s, la_r, lb_s, lb_r, lc_s, lc_r, g_s, g_r,
    r1x_s, r1x_r, r1y_s, r1y_r, r2x_s, r2x_r, r2y_s, r2y_r, f_s, f_r,
):
    t = lax.axis_index("tok")
    v = lax.axis_index("voc")
    z = v // 16
    p = v % 16
    y = p // 4
    x = p % 4
    c = t // 2
    h = t % 2
    sib = c * 2 + (1 - h)
    cross = (1 - c) * 2 + h
    diag = (1 - c) * 2 + (1 - h)
    tz = t * 4 + z

    def plane_peer(k):
        return (t, z * 16 + lax.rem(p + k, 16))

    def tz_peer(k):
        q = lax.rem(tz + k, 16)
        return (q // 4, (q % 4) * 16 + p)

    def remote(src, dst, ss, rs, dev):
        return pltpu.make_async_remote_copy(
            src_ref=src, dst_ref=dst, send_sem=ss, recv_sem=rs, device_id=dev, device_id_type=MESH
        )

    def arrived(ref, sem):
        pltpu.make_async_copy(ref, ref, sem).wait()

    bar = pltpu.get_barrier_semaphore()

    def greet(k, _):
        pl.semaphore_signal(bar, inc=1, device_id=plane_peer(k), device_id_type=MESH)
        pl.semaphore_signal(bar, inc=1, device_id=tz_peer(k), device_id_type=MESH)
        return 0

    lax.fori_loop(1, 16, greet, 0)

    c_own = pltpu.make_async_copy(head.at[:, pl.ds(mult(COLS * t, COLS), COLS)], hcols.at[t], loc.at[0])
    c_hid = pltpu.make_async_copy(hid, hid_all.at[pl.ds(mult(TG * t, TG), TG)], loc.at[1])
    order = (t, sib, cross, diag)
    c_heads = [
        pltpu.make_async_copy(
            head.at[:, pl.ds(mult(COLS * dev, COLS), COLS)], headv.at[:, pl.ds(COLS * j, COLS)], loc.at[5 + j]
        )
        for j, dev in enumerate(order)
    ]
    c_tl = pltpu.make_async_copy(teach, tloc, loc.at[3])
    c_ta = pltpu.make_async_copy(teach.at[:, p], ta.at[p // 2, p % 2], loc.at[4])
    c_q = pltpu.make_async_copy(qual_hbm, qual, loc.at[10])
    for cp in (c_hid, c_own, c_tl, c_ta, c_q, *c_heads):
        cp.start()

    pl.semaphore_wait(bar, 30)

    def piece(group, q):
        return (
            pl.ds(mult(TG * group + 16 * (q // 2), 16), 16),
            pl.ds(mult(1792 * (q % 2), 128), 1792),
        )

    pr, pc = piece(0, p)
    mr, mc = piece(t, p)
    znb = lax.rem(z + 2 * c + 3, 4)
    h_cross = remote(
        hid.at[pr, pc], hid_all.at[mr, mc], hid_s.at[0], hid_r.at[0], (cross, znb * 16 + p)
    )
    h_cross.start()
    h_pair = remote(
        hid.at[pl.ds(128, 128)], hid_all.at[pl.ds(mult(TG * t + 128, 128), 128)],
        hid_s.at[1], hid_r.at[1], (cross, znb * 16 + p),
    )
    h_sib = remote(
        hid, hid_all.at[pl.ds(mult(TG * t, TG), TG)], hid_s.at[2], hid_r.at[2], (sib, v)
    )
    heads = []
    for i, (r0, rn) in enumerate(CHUNKS):
        for j, dev in enumerate((cross, diag, sib)):
            heads.append(
                remote(
                    head.at[pl.ds(r0, rn), pl.ds(mult(COLS * dev, COLS), COLS)],
                    hcols.at[t, pl.ds(r0, rn)],
                    head_s.at[i, j], head_r.at[t, i], (dev, v),
                )
            )
    for cp in heads[:3]:
        cp.start()
    h_pair.start()
    h_sib.start()
    for cp in heads[3:]:
        cp.start()

    xr, xc = piece(cross, p)
    arrived(hid_all.at[xr, xc], hid_r.at[0])

    def spread_copy(k):
        return remote(
            hid_all.at[xr, xc], hid_all.at[xr, xc], bc_s.at[k - 1], bc_r.at[k - 1], plane_peer(k)
        )

    def ta_copy(k):
        q = lax.rem(p + k, 16)
        return remote(
            teach.at[:, q], ta.at[p // 2, p % 2], ta_s.at[k - 1], ta_r.at[k - 1], plane_peer(k)
        )

    def start_spread(k, _):
        spread_copy(k).start()
        return 0

    def start_ta(k, _):
        ta_copy(k).start()
        return 0

    lax.fori_loop(1, 16, start_spread, 0)
    lax.fori_loop(1, 16, start_ta, 0)

    c_tl.wait()

    def tl_tile(i):
        return tloc[i // 4, pl.ds(mult((i % 4) * 4, 4), 4)].astype(F32)

    def top_step(i, m):
        return jnp.maximum(m, jnp.max(tl_tile(i), axis=(0, 1)))

    top16 = lax.fori_loop(0, 16, top_step, jnp.full((16, 128), -jnp.inf, F32))
    top16 = jnp.max(top16, axis=1, keepdims=True)
    top4 = jnp.maximum(jnp.maximum(top16[0:4], top16[4:8]), jnp.maximum(top16[8:12], top16[12:16]))
    top16 = jnp.concatenate([top4] * 4, axis=0)
    top_full = jnp.broadcast_to(top16, (16, 128))

    def sum_step(i, s):
        return s + jnp.sum(jnp.exp(tl_tile(i) - top_full), axis=(0, 1))

    sum16 = lax.fori_loop(0, 16, sum_step, jnp.zeros((16, 128), F32))
    sum16 = jnp.sum(sum16, axis=1, keepdims=True)
    sum4 = sum16[0:4] + sum16[4:8] + sum16[8:12] + sum16[12:16]
    lse4 = top4 + jnp.log(sum4)
    lane = lax.broadcasted_iota(jnp.int32, (1, 128), 1)
    low = lane < 64
    trow = jnp.zeros((1, 128), F32)
    for r in range(4):
        trow = jnp.where(lane == 4 * p + r, jnp.broadcast_to(lse4[r : r + 1], (1, 128)), trow)
    row_a[...] = trow

    def swap(a):
        return pltpu.roll(a, 64, len(a.shape) - 1)

    def t1_copy(k):
        return remote(row_a, got_t.at[k - 1], t1_s.at[k - 1], t1_r.at[k - 1], plane_peer(k))

    def t2_copy(k):
        return remote(tq.at[tz], tq.at[tz], t2_s.at[k - 1], t2_r.at[k - 1], tz_peer(k))

    def start_t1(k, _):
        t1_copy(k).start()
        return 0

    def start_t2(k, _):
        t2_copy(k).start()
        return 0

    lax.fori_loop(1, 16, start_t1, 0)

    def clear(i, _):
        acc[pl.ds(mult(i * 64, 64), 64), :] = jnp.zeros((64, 2048), F32)
        return 0

    lax.fori_loop(0, 14, clear, 0)

    def wait_t1(k, _):
        arrived(got_t.at[k - 1], t1_r.at[k - 1])
        return 0

    lax.fori_loop(1, 16, wait_t1, 0)
    tl_row = row_a[...] + jnp.sum(got_t[...], axis=0)
    c_q.wait()
    q_row = qual[pl.ds(z // 2, 1), :]
    weight = LOSS_SCALE * jnp.where(lax.rem(z, 2) == 0, q_row, swap(q_row))
    tq[tz] = jnp.where(low, tl_row - jnp.log(weight), swap(weight))
    lax.fori_loop(1, 16, start_t2, 0)

    gx = mult(TG * cross, TG)

    def wait_spread(k, _):
        ar, ac = piece(cross, lax.rem(p + 16 - k, 16))
        arrived(hid_all.at[ar, ac], bc_r.at[k - 1])
        return 0

    lax.fori_loop(1, 16, wait_spread, 0)
    fwd1 = remote(
        hid_all.at[pl.ds(gx, 128)], hid_all.at[pl.ds(gx, 128)], hid_s.at[3], hid_r.at[3], (sib, v)
    )
    fwd1.start()
    gx2 = mult(TG * cross + 128, 128)
    arrived(hid_all.at[pl.ds(gx2, 128)], hid_r.at[1])
    fwd2 = remote(
        hid_all.at[pl.ds(gx2, 128)], hid_all.at[pl.ds(gx2, 128)], hid_s.at[4], hid_r.at[4], (sib, v)
    )
    fwd2.start()
    c_hid.wait()
    arrived(hid_all.at[pl.ds(mult(TG * sib, TG), TG)], hid_r.at[2])
    arrived(hid_all.at[pl.ds(mult(TG * diag, 128), 128)], hid_r.at[3])
    arrived(hid_all.at[pl.ds(mult(TG * diag + 128, 128), 128)], hid_r.at[4])

    def multiply(slot, r0, rn, first):
        base = mult(DS * slot + r0, 128)

        term = jnp.dot(
            hid_all[:, pl.ds(base, rn)], hcols[slot, pl.ds(r0, rn), :], preferred_element_type=F32
        )
        if first:
            stu[...] = term
        else:
            stu[...] += term

    def wait_head(slot, i):
        r0, rn = CHUNKS[i]
        arrived(hcols.at[slot, pl.ds(r0, rn)], head_r.at[slot, i])

    c_own.wait()
    multiply(t, 0, DS, True)
    for i in range(4):
        wait_head(sib, i)
    multiply(sib, 0, DS, False)

    def turn(i, _):
        rows = pl.ds(mult(i * 128, 128), 128)
        for j in range(7):
            block = hid_all[rows, pl.ds(mult(DS * t + 128 * j, 128), 128)]
            hid_t[128 * j : 128 * (j + 1), rows] = block.astype(F32).T.astype(BF16)
        return 0

    lax.fori_loop(0, 8, turn, 0)

    for i in range(3):
        r0, rn = CHUNKS[i]
        wait_head(cross, i)
        multiply(cross, r0, rn, False)
        wait_head(diag, i)
        multiply(diag, r0, rn, False)

    c_ta.wait()

    def wait_ta(k, _):
        q = lax.rem(p + 16 - k, 16)
        arrived(ta.at[q // 2, q % 2], ta_r.at[k - 1])
        return 0

    lax.fori_loop(1, 16, wait_ta, 0)
    def tb_copy(k):
        q = lax.rem(tz + k, 16)
        return remote(
            ta.at[:, :, q % 4, q // 4], tb.at[tz], tb_s.at[k], tb_r.at[tz], tz_peer(k)
        )

    def is_early(k):
        q = lax.rem(tz + k, 16)
        t2, zq = q // 4, q % 4
        return ((t2 // 2 != c) & (zq == znb)) | ((t2 == sib) & (zq == z))

    def start_tb(k, _):
        @pl.when(jnp.logical_not(is_early(k)))
        def _():
            tb_copy(k).start()

        return 0

    def start_early(k, _):
        @pl.when(is_early(k))
        def _():
            tb_copy(k).start()

        return 0

    lax.fori_loop(1, 16, start_early, 0)
    wait_head(cross, 3)
    wait_head(diag, 3)
    for cp in heads:
        cp.wait_send()
    lax.fori_loop(1, TB_SPLIT, start_tb, 0)
    c_tb = pltpu.make_async_copy(ta.at[:, :, z, t], tb.at[tz], tb_r.at[tz])
    c_tb.start()

    c_hx = pltpu.make_async_copy(hcols.at[cross], hxc.at[:, pl.ds(0, COLS)], loc.at[9])
    c_hx.start()
    h_hx = remote(hcols.at[diag], hxc.at[:, pl.ds(COLS, COLS)], hx_s.at[0], hx_r.at[0], (sib, v))
    h_hx.start()

    r0, rn = CHUNKS[3]
    multiply(cross, r0, rn, False)
    multiply(diag, r0, rn, False)

    def stats(b, _):
        rows = pl.ds(mult(b * BLK, BLK), BLK)
        val = stu[rows, :]
        top = jnp.max(val, axis=1, keepdims=True)
        e = jnp.exp(val - top)
        stu[rows, :] = e
        tot = jnp.sum(e, axis=1, keepdims=True)
        both = jnp.where(jnp.broadcast_to(low, (BLK, BLK)), top, tot).T
        m_row, s_row = both[0:1, :], both[64:65, :]
        st[2 * b] = jnp.where(low, m_row, swap(s_row))
        st[2 * b + 1] = jnp.where(low, swap(m_row), s_row)
        return 0

    lax.fori_loop(0, NB, stats, 0, unroll=4)

    def la_copy(k):
        return remote(
            st.at[lax.rem(p + k, 16)], got_a.at[k - 1], la_s.at[k - 1], la_r.at[k - 1], plane_peer(k)
        )

    def lb_copy(k):
        return remote(row_b, got_b.at[k - 1], lb_s.at[k - 1], lb_r.at[k - 1], tz_peer(k))

    def lc_copy(k):
        return remote(full.at[p], full.at[p], lc_s.at[k - 1], lc_r.at[k - 1], plane_peer(k))

    def start_la(k, _):
        la_copy(k).start()
        return 0

    def start_lb(k, _):
        lb_copy(k).start()
        return 0

    def start_lc(k, _):
        lc_copy(k).start()
        return 0

    def combine(mine, got):
        top = jnp.maximum(mine, jnp.max(got, axis=0))
        tot = swap(mine) * jnp.exp(mine - top) + jnp.sum(swap(got) * jnp.exp(got - top[None]), axis=0)
        return jnp.where(low, top, swap(tot))

    lax.fori_loop(1, 16, start_la, 0)

    def wait_la(k, _):
        arrived(got_a.at[k - 1], la_r.at[k - 1])
        return 0

    lax.fori_loop(1, 16, wait_la, 0)
    row_b[...] = combine(st[p], got_a[...])
    lax.fori_loop(1, 16, start_lb, 0)
    lax.fori_loop(TB_SPLIT, 16, start_tb, 0)

    def wait_lb(k, _):
        arrived(got_b.at[k - 1], lb_r.at[k - 1])
        return 0

    lax.fori_loop(1, 16, wait_lb, 0)
    full[p] = combine(row_b[...], got_b[...])
    lax.fori_loop(1, 16, start_lc, 0)

    def wait_t2(k, _):
        q = lax.rem(tz + 16 - k, 16)
        arrived(tq.at[q], t2_r.at[k - 1])
        return 0

    def wait_lc(k, _):
        q = lax.rem(p + 16 - k, 16)
        arrived(full.at[q], lc_r.at[k - 1])
        return 0

    lax.fori_loop(1, 16, wait_t2, 0)
    lax.fori_loop(1, 16, wait_lc, 0)
    scale[...] = swap(tq[...]) * jnp.exp(st[...] - full[...]) / swap(full[...])

    def g_copy(b, j, src, dst, dev):
        rows = pl.ds(mult(b * BLK, BLK), BLK)
        return remote(
            gs.at[rows, pl.ds(COLS * src, COLS)], gs.at[rows, pl.ds(COLS * dst, COLS)],
            g_s.at[b, j], g_r.at[b, j], (dev, v),
        )

    def g_cross(b):
        return g_copy(b, 0, 0, 2, cross)

    def g_sib(b):
        return g_copy(b, 1, 0, 1, sib)

    def g_fwd(b):
        return g_copy(b, 2, 2, 3, sib)

    def g_wait(b, j):
        slot = (2, 1, 3)[j]
        rows = pl.ds(mult(b * BLK, BLK), BLK)
        arrived(gs.at[rows, pl.ds(COLS * slot, COLS)], g_r.at[b, j])

    sub = lax.broadcasted_iota(jnp.int32, (16, 8, 128), 1) < 4

    def make_grads(b, _):
        rows = pl.ds(mult(b * BLK, BLK), BLK)
        for s in range(2):
            arrived(tb.at[2 * b + s], tb_r.at[2 * b + s])
        even = tb[pl.ds(mult(2 * b, 2), 2), :, 0].astype(F32).reshape(16, 16, 128)
        odd = tb[pl.ds(mult(2 * b, 2), 2), :, 1].astype(F32).reshape(16, 16, 128)
        sc_row = jnp.where(low, scale[2 * b], swap(scale[2 * b + 1]))
        tl_row = jnp.where(low, tq[2 * b], swap(tq[2 * b + 1]))
        sc = jnp.broadcast_to(sc_row, (BLK, BLK)).T
        tl = jnp.broadcast_to(tl_row, (BLK, BLK)).T
        for q in range(4):
            half = slice(8 * (q // 2), 8 * (q // 2) + 8)
            lo, hi = even[:, half], odd[:, half]
            if q % 2 == 0:
                mixed = jnp.where(sub, lo, pltpu.roll(hi, 4, 1))
            else:
                mixed = jnp.where(sub, pltpu.roll(lo, 4, 1), hi)
            teacher = mixed.reshape(BLK, 128)
            e = stu[rows, 128 * q : 128 * (q + 1)]
            g = e * sc - jnp.exp(teacher - tl)
            gs[rows, 128 * q : 128 * (q + 1)] = g.astype(BF16)
        g_sib(b).start()

        @pl.when(b < NB - NX)
        def _():
            g_cross(b).start()

        return 0

    lax.fori_loop(0, NB, make_grads, 0)
    for b in range(NB - NX, NB):
        g_cross(b).start()
    c_hx.wait()
    arrived(hxc.at[:, pl.ds(COLS, COLS)], hx_r.at[0])
    for cp in c_heads:
        cp.wait()

    ca = x + h * (y - x)
    cb = y + h * (x - y)

    def line_a(k):
        return (t, z * 16 + (1 - h) * (y * 4 + lax.rem(x + k, 4)) + h * (lax.rem(y + k, 4) * 4 + x))

    def line_b(k):
        return (t, z * 16 + h * (y * 4 + lax.rem(x + k, 4)) + (1 - h) * (lax.rem(y + k, 4) * 4 + x))

    def copies1(b, k):
        i = k - 1
        return (
            remote(zx.at[b, i], r1x.at[b, i], r1x_s.at[b, i], r1x_r.at[b, i], line_a(k)),
            remote(zy.at[b, i], r1y.at[b, i], r1y_s.at[b, i], r1y_r.at[b, i], line_b(k)),
        )

    def copies2(b, k):
        i = k - 1
        return (
            remote(z2x.at[b, i], r2x.at[b, i], r2x_s.at[b, i], r2x_r.at[b, i], line_b(k)),
            remote(z2y.at[b, i], r2y.at[b, i], r2y_s.at[b, i], r2y_r.at[b, i], line_a(k)),
        )

    def block_of(n):
        return n - NX * (n // NB)

    def run_of(n):
        return t + (n // NB) * (cross - t)

    def copy3(n):
        b = block_of(n)
        at = (n // NB, z, lax.rem(b, 2))
        return remote(s2.at[n], fin.at[at], f_s.at[n], f_r.at[at], (b // 2, run_of(n) * 16 + p))

    def mine(n):
        return (block_of(n) // 2 == t) & (run_of(n) == z)

    def hand_on(b):
        g_wait(b, 0)
        g_fwd(b).start()

    def dot_t(a, b):
        return lax.dot_general(a, b, (((1,), (1,)), ((), ())), preferred_element_type=F32)

    def step1(b):
        rows = pl.ds(mult(b * BLK, BLK), BLK)
        g_wait(b, 1)
        g_wait(b, 2)
        keep(b, dot_t(headv[...], gs[rows, :]), 0)
        spread(b)

    def alone_blocks():
        for b in range(NB - NX, NB):
            g_wait(b, 1)
        for n, rows_of in ((NB - NX, headv), (NB, hxc)):
            for m in range(2):
                out = dot_t(
                    rows_of[448 * m : 448 * (m + 1), 0 : 2 * COLS],
                    gs[BLK * (NB - NX) :, 0 : 2 * COLS],
                )
                for k in range(NX):
                    keep(n + k, out[:, BLK * k : BLK * (k + 1)], 2 * m)
        for k in range(NX):
            spread(NB - NX + k)
            spread(NB + k)

    def keep(n, out, begin):
        for i in range(begin, begin + out.shape[0] // (4 * ROWS)):
            for j in range(4):
                first = ROWS * (4 * (i - begin) + j)
                pb[n, i + h * (j - i), j + h * (i - j)] = out[first : first + ROWS]

    def spread(b):
        for k in (2, 1, 3):
            to_a, to_b = lax.rem(ca + k, 4), lax.rem(cb + k, 4)
            zx[b, k - 1] = pb[b, :, to_a, 0:32].reshape(128, BLK).astype(BF16)
            zy[b, k - 1] = pb[b, to_b, :, 32:56].reshape(96, BLK).astype(BF16)
            for cp in copies1(b, k):
                cp.start()

    def step2(b):
        for i in range(3):
            arrived(r1x.at[b, i], r1x_r.at[b, i])
            arrived(r1y.at[b, i], r1y_r.at[b, i])
        from_a = (r1x[b, 0].astype(F32) + r1x[b, 1].astype(F32)) + r1x[b, 2].astype(F32)
        from_b = (r1y[b, 0].astype(F32) + r1y[b, 1].astype(F32)) + r1y[b, 2].astype(F32)
        s1x[b] = pb[b, :, ca, 0:32] + from_a.reshape(4, 32, BLK)
        s1y[b] = pb[b, cb, :, 32:56] + from_b.reshape(4, 24, BLK)
        for k in (2, 1, 3):
            z2x[b, k - 1] = s1x[b, lax.rem(cb + k, 4)].astype(BF16)
            tail = jnp.zeros((8, BLK), F32)
            z2y[b, k - 1] = jnp.concatenate([s1y[b, lax.rem(ca + k, 4)], tail], axis=0).astype(BF16)
            for cp in copies2(b, k):
                cp.start()

    def step3(b):
        for k in (1, 2, 3):
            arrived(r2x.at[b, k - 1], r2x_r.at[b, k - 1])
            arrived(r2y.at[b, k - 1], r2y_r.at[b, k - 1])
        from_b = (r2x[b, 0].astype(F32) + r2x[b, 1].astype(F32)) + r2x[b, 2].astype(F32)
        from_a = (r2y[b, 0].astype(F32) + r2y[b, 1].astype(F32)) + r2y[b, 2].astype(F32)
        s2[b, 0:32] = (s1x[b, cb] + from_b).astype(BF16)
        pad = jnp.zeros((8, BLK), F32)
        s2[b, 32:64] = jnp.concatenate([s1y[b, ca] + from_a[0:24], pad], axis=0).astype(BF16)

        @pl.when(mine(b))
        def _():
            fin[b // NB, z, lax.rem(block_of(b), 2)] = s2[b]

        @pl.when(jnp.logical_not(mine(b)))
        def _():
            copy3(b).start()

    def group_term(g, i, half):
        term = jnp.dot(
            hid_t[128 * i : 128 * (i + 1), pl.ds(mult(g * TG, TG), TG)],
            gs[pl.ds(mult(g * TG, TG), TG), 1024 * half : 1024 * (half + 1)],
            preferred_element_type=F32,
        )
        return term.astype(BF16).astype(F32)

    def add_group(g, half):
        for i in range(7):
            rows = slice(128 * i, 128 * (i + 1))
            cols = slice(1024 * half, 1024 * (half + 1))
            new = acc[rows, cols] + group_term(g, i, half)
            acc[rows, cols] = new
            out = new.astype(BF16)
            for j in range(2):
                at = mult(COLS * order[2 * half + j], COLS)
                gh[rows, pl.ds(at, COLS)] = out[:, COLS * j : COLS * (j + 1)]

    def when(condition, step, *args):
        @pl.when(condition)
        def _():
            step(*args)

    alone_blocks()
    hand_on(0)

    def early2(i):
        step2(NB - NX + i)
        step2(NB + i)

    def early3(i):
        step3(NB - NX + i)
        step3(NB + i)

    def late_waits():
        g_wait(6, 2)
        g_wait(7, 2)

    def block(i, _):
        when(i < 5, step1, i)
        when(i < 4, hand_on, i + 1)
        when((i > 1) & (i < 5), early2, i - 2)
        when((i > 2) & (i < 8), step2, i - 3)
        when(i == 5, hand_on, 5)
        when(i == 6, g_wait, 5, 2)
        when(i == 8, step3, 3)
        when(i == 8, step3, 4)
        when(i == 8, hand_on, 7)
        when(i == 8, late_waits)
        g = (i - 1 - i // 5) // 2
        first = (i == 1) | (i == 4) | (i == 6) | (i == 8)
        when(first, add_group, g, 0)
        when((i > 0) & (i != 3) & jnp.logical_not(first), add_group, g, 1)
        when((i > 4) & (i < 8), early3, i - 5)
        when(i == 6, step3, 0)
        when(i == 7, step3, 1)
        when(i == 7, step3, 2)
        when(i == 7, hand_on, 6)
        return 0

    lax.fori_loop(0, 10, block, 0)

    for cp in (h_cross, h_pair, h_sib, fwd1, fwd2, h_hx):
        cp.wait_send()

    def drain(k, _):
        spread_copy(k).wait_send()
        ta_copy(k).wait_send()
        tb_copy(k).wait_send()
        t1_copy(k).wait_send()
        t2_copy(k).wait_send()
        la_copy(k).wait_send()
        lb_copy(k).wait_send()
        lc_copy(k).wait_send()
        return 0

    lax.fori_loop(1, 16, drain, 0)

    def drain_blocks(b, _):
        g_cross(b).wait_send()
        g_sib(b).wait_send()
        g_fwd(b).wait_send()
        return 0

    def drain_sums(n, _):
        for k in (1, 2, 3):
            for cp in copies1(n, k) + copies2(n, k):
                cp.wait_send()

        @pl.when(jnp.logical_not(mine(n)))
        def _():
            copy3(n).wait_send()

        return 0

    lax.fori_loop(0, NS, drain_sums, 0)
    lax.fori_loop(0, NB, drain_blocks, 0)

    for half in range(2):
        cols = slice(128 * half, 128 * (half + 1))

        def part(source, k, half=half):
            return fin[source, k, half].astype(F32)[0:ROWS]

        for k in range(4):

            @pl.when(jnp.logical_not((t == z) & (z == k)))
            def _():
                arrived(fin.at[0, k, half], f_r.at[0, k, half])

        near = (part(0, 0) + part(0, 1)) + (part(0, 2) + part(0, 3))
        alone = 2 * t + half >= NB - NX

        @pl.when(jnp.logical_not(alone))
        def _():
            hg[:, cols] = near.astype(BF16)

        @pl.when(alone)
        def _():
            for k in range(4):

                @pl.when(jnp.logical_not((lax.rem(t + 2, 4) == z) & (z == k)))
                def _():
                    arrived(fin.at[1, k, half], f_r.at[1, k, half])

            rest = (part(1, 0) + part(1, 1)) + (part(1, 2) + part(1, 3))
            hg[:, cols] = (near + rest).astype(BF16)


def hand_over(hg_in, gh_in, hg, gh, sem):
    copies = [pltpu.make_async_copy(hg_in, hg, sem.at[7])]
    for i in range(7):
        rows = pl.ds(128 * i, 128)
        copies.append(pltpu.make_async_copy(gh_in.at[rows], gh.at[rows], sem.at[i]))
    for cp in copies:
        cp.start()
    for cp in copies:
        cp.wait()


def body(hidden_states, student_head, teacher_logits, quality):
    teach = (
        teacher_logits.reshape(4, 256, 4, 128).transpose(1, 2, 0, 3).reshape(4, 16, 4, 16, 128)
    )
    hbm = pl.BlockSpec(memory_space=pltpu.HBM)
    vmem = pl.BlockSpec(memory_space=pltpu.VMEM)
    dma = pltpu.SemaphoreType.DMA
    hg, gh = pl.pallas_call(
        kernel,
        name="distill_backward",
        out_shape=(pltpu.VMEM((ROWS, TG), BF16), pltpu.VMEM((DS, 2048), BF16)),
        in_specs=[hbm, hbm, hbm, hbm],
        out_specs=(vmem, vmem),
        scratch_shapes=[
            pltpu.VMEM((TOK, D), BF16),
            pltpu.VMEM((DS, 2048), BF16),
            pltpu.VMEM((4, DS, COLS), BF16),
            pltpu.VMEM((DS, 2 * COLS), BF16),
            pltpu.VMEM((4, 16, 4, 16, 128), BF16),
            pltpu.VMEM((8, 2, 4, 4, 16, 128), BF16),
            pltpu.VMEM((16, 8, 2, 16, 128), BF16),
            pltpu.VMEM((TOK, COLS), F32),
            pltpu.VMEM((TOK, 2048), BF16),
            pltpu.VMEM((DS, TOK), BF16),
            pltpu.VMEM((DS, 2048), F32),
            pltpu.VMEM((NS, 4, 4, ROWS, BLK), F32),
            pltpu.VMEM((NS, 3, 128, BLK), BF16),
            pltpu.VMEM((NS, 3, 96, BLK), BF16),
            pltpu.VMEM((NS, 3, 128, BLK), BF16),
            pltpu.VMEM((NS, 3, 96, BLK), BF16),
            pltpu.VMEM((NS, 4, 32, BLK), F32),
            pltpu.VMEM((NS, 4, 24, BLK), F32),
            pltpu.VMEM((NS, 3, 32, BLK), BF16),
            pltpu.VMEM((NS, 3, 32, BLK), BF16),
            pltpu.VMEM((NS, 3, 32, BLK), BF16),
            pltpu.VMEM((NS, 3, 32, BLK), BF16),
            pltpu.VMEM((NS, 64, BLK), BF16),
            pltpu.VMEM((2, 4, 2, 64, BLK), BF16),
            pltpu.VMEM((2, 128), F32),
            pltpu.VMEM((1, 128), F32),
            pltpu.VMEM((15, 1, 128), F32),
            pltpu.VMEM((16, 1, 128), F32),
            pltpu.VMEM((16, 1, 128), F32),
            pltpu.VMEM((15, 1, 128), F32),
            pltpu.VMEM((1, 128), F32),
            pltpu.VMEM((15, 1, 128), F32),
            pltpu.VMEM((16, 1, 128), F32),
            pltpu.VMEM((16, 1, 128), F32),
            dma((11,)),
            dma((4, 3)), dma((4, 4)),
            dma((1,)), dma((1,)),
            dma((5,)), dma((5,)),
            dma((15,)), dma((15,)),
            dma((15,)), dma((15,)),
            dma((16,)), dma((16,)),
            dma((15,)), dma((15,)),
            dma((15,)), dma((15,)),
            dma((15,)), dma((15,)),
            dma((15,)), dma((15,)),
            dma((15,)), dma((15,)),
            dma((NB, 3)), dma((NB, 3)),
            dma((NS, 3)), dma((NS, 3)),
            dma((NS, 3)), dma((NS, 3)),
            dma((NS, 3)), dma((NS, 3)),
            dma((NS, 3)), dma((NS, 3)),
            dma((NS,)), dma((2, 4, 2)),
        ],
        compiler_params=pltpu.CompilerParams(
            collective_id=0, has_side_effects=True, vmem_limit_bytes=55 * 2**20
        ),
        cost_estimate=pl.CostEstimate(
            flops=3 * 2 * TOK * DS * 2048, bytes_accessed=15 * 2**20, transcendentals=2**21
        ),
    )(hidden_states, student_head, teach, quality.reshape(2, 128))
    hg, gh = pl.pallas_call(
        hand_over,
        name="results",
        out_shape=(
            jax.ShapeDtypeStruct((ROWS, TG), BF16),
            jax.ShapeDtypeStruct((DS, 2048), BF16),
        ),
        in_specs=[vmem, vmem],
        out_specs=(hbm, hbm),
        scratch_shapes=[dma((8,))],
        compiler_params=pltpu.CompilerParams(vmem_limit_bytes=2**20),
    )(
        pltpu.with_memory_space_constraint(hg, pltpu.VMEM),
        pltpu.with_memory_space_constraint(gh, pltpu.VMEM),
    )
    return hg.T, gh


def solution(mesh):
    return jax.shard_map(
        body,
        mesh=mesh,
        in_specs=(P("tok", None), P("tok", "voc"), P(("tok", "voc"), None), P("tok")),
        out_specs=(P("tok", "voc"), P("tok", "voc")),
        check_vma=False,
    )
```
